512 devices in a mesh: table: 128 (over z, x, core), seq: 4 (over y).
Axes of the slice: x: 4, y: 4, z: 16, core: 2. Of those that a mesh axis runs over, the one named last changes fastest.
Arguments:
- embedding_table: bfloat16 [65536, 512], P('table'), may hold values from -6 to 6
- project_in: bfloat16 [512, 2048], replicated, may hold values from -0.25 to 0.25
- project_out: bfloat16 [512, 512], replicated, may hold values from -0.25 to 0.25
- row_owner: int32 [65536, 1], P(('table', 'seq')), may hold values from 0 to 127; in each aligned block of 128 rows (0 to 127, 128 to 255, ...) at most 2 rows name the same one
- row_offset: int32 [65536], P(('table', 'seq')), may hold values from 0 to 511
- user_lengths: int32 [128, 3], P('table'), may hold values from 1 to 256, 512 in all within a row
- upstream: bfloat16 [65536, 512], P(('table', 'seq')), may hold values from -6 to 6
Outputs:
- layer_out: bfloat16 [65536, 512], P(('table', 'seq'))
- table_grad: float32 [65536, 512], P('table')
The draws below stay inside these ranges and needn't reach their ends.
Inputs may be any that keep to these rules, and one draw needn't show every extreme that they name: `row_owner`: in each aligned block of 128 rows (the rows of one device) no owner is named by more than 2 rows, a bound that some block reaches. `user_lengths`: each row sums to 512.
All inputs are finite; a program needn't handle non-finite values.
Results may differ from the reference program's by a relative error of at most 0.0064.
Values may be sent and summed in bfloat16 or wider, within the bound.
A program may use at most 64 MiB of HBM per device.

```python
import math
from functools import partial
import jax
import jax.numpy as jnp
import numpy as np
from jax import lax

D = 512
HEADS = 4
HEAD_DIM = 128
TOK_DEV = 128
ROWS_DEV = 512
USERS = 3
GL = 512
TOKENS = 65536
ROWS = 65536
CAP = 2
N_TABLE = 128


def with_ends(entries, key, smallest, high):
    shape = entries.shape
    spot = [jax.random.randint(jax.random.fold_in(key, axis), (), 0, shape[axis]) for axis in range(len(shape))]
    entries = entries.at[tuple(spot)].set(smallest)
    longest = shape.index(max(shape))
    spot[longest] = (spot[longest] + 1) % shape[longest]
    return entries.at[tuple(spot)].set(high)


def level_of(key, dims, shards, least, largest):
    loudness, own = 1.0, jax.random.fold_in(key, 6)
    for dim, blocks in shards:
        draws = jnp.exp(jax.random.uniform(jax.random.fold_in(own, dim), (blocks,), jnp.float32, least / len(shards), largest / len(shards)))
        loudness = loudness * jnp.repeat(draws, dims[dim] // blocks).reshape([-1 if axis == dim else 1 for axis in range(len(dims))])
    return loudness


def split_up(amount, total, most, lean):
    portions = [(1 << 20) // math.isqrt(standing ** lean) + 1 for standing in range(2, amount + 1)]
    rest, holding = total - most - (amount - 1), [1] * (amount - 1)
    while rest > 0:
        candidates = [i for i in range(amount - 1) if holding[i] < most]
        pool, budget = sum([portions[i] for i in candidates]), rest
        for i in candidates:
            more = min(most - holding[i], max(1, budget * portions[i] // pool), rest)
            holding[i] = holding[i] + more
            rest = rest - more
    return np.array([most] + holding)


def uneven_parts(rng, count, total, bound, skew):
    if count == 2:
        one = jax.random.randint(rng, (), max(1, total - bound), min(bound, total - 1) + 1)
        return jnp.stack([one, total - one])
    sizes = jnp.asarray(split_up(count, total, bound, skew), jnp.int32)
    twos = (count - 1) // 2
    source_of, receiver = sizes[1:1 + 2 * twos:2], sizes[2:2 + 2 * twos:2]
    margin = jnp.minimum(source_of - 1, bound - receiver)
    shifted = jax.random.randint(jax.random.fold_in(rng, 1), (twos,), 0, 1 << 20) % (margin + 1)
    sizes = sizes.at[1:1 + 2 * twos:2].set(source_of - shifted).at[2:2 + 2 * twos:2].set(receiver + shifted)
    return sizes[jax.random.permutation(jax.random.fold_in(rng, 2), count)]


def routed_block(key, own, number, rows, number_of, top, reach, lean):
    sequence = jax.random.permutation(key, number_of)
    crowded, usual = portions_of(number_of, rows * top, reach, lean, True), portions_of(number_of, rows * top, reach, lean, False)
    places = jnp.arange(number_of)

    def named(tallies, offset_by):
        used = int((tallies > 0).sum())
        fixed = max(1, used // 4)
        passed = fixed + (places - fixed + offset_by * (used - fixed)) % max(1, number_of - fixed)
        return jnp.zeros((number_of,), jnp.int32).at[sequence[jnp.where(places < fixed, places, passed)]].set(jnp.asarray(tallies, jnp.int32))

    tallies = jnp.where(number % 4 == 0, named(crowded, number // 4), named(usual, number - number // 4 - 1))
    mixed = jax.random.permutation(jax.random.fold_in(own, 3), number_of)
    donor, taker = mixed[0:number_of // 2 * 2:2], mixed[1:number_of // 2 * 2:2]
    room = jnp.minimum(tallies[donor] - 1, reach - tallies[taker]) // 2
    room = jnp.where((donor == sequence[0]) | (taker == sequence[0]) | (tallies[taker] == 0), 0, jnp.maximum(room, 0))
    passed = jax.random.randint(jax.random.fold_in(own, 4), (number_of // 2,), 0, 1 << 20) % (room + 1)
    tallies = tallies.at[donor].add(-passed).at[taker].add(passed)
    members = jnp.searchsorted(jnp.cumsum(tallies), jnp.arange(rows * top), side="right").astype(jnp.int32)
    listing = members.reshape(top, rows).T
    listing = listing[jax.random.permutation(jax.random.fold_in(own, 1), rows)]
    offset_by = jax.random.randint(jax.random.fold_in(own, 2), (rows, 1), 0, top)
    return jnp.take_along_axis(listing, (jnp.arange(top)[None, :] + offset_by) % top, axis=1)


def portions_of(number_of, total, bound, lean, full):
    weights = [(1 << 20) // math.isqrt(grade ** lean) + 1 for grade in range(1, number_of + 1)]
    largest = bound if full else min(bound, max(-(-total // number_of), total * weights[0] // sum(weights)))
    least = 1 if total - largest >= number_of - 1 else 0
    holding, spare = [largest] + [least] * (number_of - 1), total - largest - least * (number_of - 1)
    while spare > 0:
        free = [i for i in range(1, number_of) if holding[i] < largest] or [i for i in range(1, number_of) if holding[i] < bound]
        whole, left = sum([weights[i] for i in free]), spare
        for i in free:
            extra = min(bound - holding[i], max(1, left * weights[i] // whole), spare)
            holding[i] = holding[i] + extra
            spare = spare - extra
    return np.array(holding)


def bell_draw(rng, dims, spread, bound, split=(), kind=jnp.bfloat16):
    entries = jax.random.normal(rng, dims, jnp.float32) * spread
    if len(split) > 0:
        entries = level_of(rng, dims, split, -0.22, 0.18) * entries
    return jnp.clip(entries, min=-bound, max=bound).astype(kind)


def setup_inputs(seed: int = 0) -> dict:
    splits = jax.random.split(jax.random.key(seed), 8)
    embedding_table = bell_draw(splits[0], (ROWS, D), 1.0, 6.0, ((0, 128),))
    project_in = bell_draw(splits[1], (D, 4 * D), D ** -0.5, 0.25)
    project_out = bell_draw(splits[2], (D, D), D ** -0.5, 0.25)
    row_owner_keys = jax.random.split(jax.random.fold_in(splits[3], 1), TOKENS // TOK_DEV)
    row_owner_turns = jax.random.permutation(jax.random.fold_in(splits[3], 3), TOKENS // TOK_DEV)
    row_owner = jax.vmap(lambda own, number: routed_block(jax.random.fold_in(splits[3], 2), own, number, TOK_DEV, N_TABLE, 1, CAP, 2))(row_owner_keys, row_owner_turns).reshape((TOKENS, 1))
    row_offset = with_ends(jax.random.randint(splits[4], (TOKENS,), 0, ROWS_DEV), jax.random.fold_in(splits[4], 1), 0, ROWS_DEV - 1).astype(jnp.int32)
    user_lengths = jax.vmap(lambda own: uneven_parts(own, USERS, GL, GL // 2, 2))(jax.random.split(splits[5], N_TABLE)).reshape((N_TABLE, USERS)).astype(jnp.int32)
    upstream = bell_draw(splits[6], (TOKENS, D), 1.0, 6.0, ((0, 512),))
    return dict(embedding_table=embedding_table, project_in=project_in, project_out=project_out, row_owner=row_owner, row_offset=row_offset, user_lengths=user_lengths, upstream=upstream)


EPS = 1e-05

def silu_slope(inputs):
    logistic = jax.nn.sigmoid(inputs)
    return logistic * (1.0 + inputs * (1.0 - logistic))

def normalize(inputs):
    center = inputs - lax.optimization_barrier(jnp.mean(inputs, axis=-1, keepdims=True))
    inv_scale = lax.rsqrt(lax.optimization_barrier(jnp.mean(center * center, axis=-1, keepdims=True)) + EPS)
    return (center * inv_scale, inv_scale)

def normalize_back(grad_in, normed, inv_scale):
    return inv_scale * (grad_in - lax.optimization_barrier(jnp.mean(grad_in, axis=-1, keepdims=True)) - normed * lax.optimization_barrier(jnp.mean(grad_in * normed, axis=-1, keepdims=True)))

def allowed_pairs(query_index, key_index, bounds):
    query_user = lax.optimization_barrier(jnp.sum((query_index[:, None] >= bounds[None, :]).astype(jnp.int32), axis=1))
    key_user = lax.optimization_barrier(jnp.sum((key_index[:, None] >= bounds[None, :]).astype(jnp.int32), axis=1))
    same_user = (query_user[:, None] == key_user[None, :]) & (key_index[None, :] <= query_index[:, None])
    return same_user.astype(jnp.float32)

def split_heads(matrix):
    return matrix.astype(jnp.float32).reshape(matrix.shape[0], HEADS, HEAD_DIM)

def group_pass(project_in, project_out, packed):
    embedded, lengths, upstream = packed
    length = embedded.shape[0]
    positions = jnp.arange(length, dtype=jnp.int32)
    bounds = jnp.cumsum(lengths).astype(jnp.int32)
    normed, inv_scale = normalize(embedded.astype(jnp.float32))
    projected = jnp.dot(normed.astype(jnp.bfloat16), project_in, preferred_element_type=jnp.float32)
    activated = jax.nn.silu(projected).astype(jnp.bfloat16)
    gate_u = activated[:, :D]
    head_v = split_heads(activated[:, D:2 * D])
    head_q = split_heads(activated[:, 2 * D:3 * D])
    head_k = split_heads(activated[:, 3 * D:])
    score_scale = HEAD_DIM ** (-0.5)
    scores = jnp.einsum('qhe,khe->hqk', head_q, head_k) * score_scale
    allowed = allowed_pairs(positions, positions, bounds)[None]
    weights = (jax.nn.silu(scores) * allowed).astype(jnp.bfloat16)
    attended = jnp.einsum('hqk,khe->qhe', weights.astype(jnp.float32), head_v).reshape(length, D)
    attn_normed, attn_inv = normalize(attended)
    gated = attn_normed * gate_u.astype(jnp.float32)
    layer_out = (embedded.astype(jnp.float32) + jnp.dot(gated.astype(jnp.bfloat16), project_out, preferred_element_type=jnp.float32)).astype(jnp.bfloat16)
    grad_gated = jnp.dot(upstream, project_out.T, preferred_element_type=jnp.float32)
    grad_gate = grad_gated * attn_normed
    grad_out = normalize_back(grad_gated * gate_u.astype(jnp.float32), attn_normed, attn_inv).astype(jnp.bfloat16)
    head_d = split_heads(grad_out)
    grad_attn = jnp.einsum('qhe,khe->hqk', head_d, head_v)
    grad_score = (grad_attn * silu_slope(scores) * allowed * score_scale).astype(jnp.bfloat16)
    grad_score_wide = grad_score.astype(jnp.float32)
    grad_query = jnp.einsum('hqk,khe->qhe', grad_score_wide, head_k).reshape(length, D)
    grad_key = jnp.einsum('hqk,qhe->khe', grad_score_wide, head_q).reshape(length, D)
    grad_value = jnp.einsum('hqk,qhe->khe', weights.astype(jnp.float32), head_d).reshape(length, D)
    grad_acts = jnp.concatenate([grad_gate, grad_value, grad_query, grad_key], axis=1)
    grad_projected = (grad_acts * silu_slope(projected)).astype(jnp.bfloat16)
    grad_normed = jnp.dot(grad_projected, project_in.T, preferred_element_type=jnp.float32)
    grad_embed = upstream.astype(jnp.float32) + normalize_back(grad_normed, normed, inv_scale)
    return (layer_out, grad_embed)

def reference(embedding_table, project_in, project_out, row_owner, row_offset, user_lengths, upstream):
    ids = (row_owner[:, 0] * ROWS_DEV + row_offset).astype(jnp.int32)
    embedded = jnp.take(embedding_table, ids, axis=0)
    packed = (embedded.reshape(N_TABLE, GL, D), user_lengths, upstream.reshape(N_TABLE, GL, D))
    outputs, grads = lax.map(partial(group_pass, project_in, project_out), packed)
    layer_out = outputs.reshape(TOKENS, D)
    table_grad = jnp.zeros((ROWS, D), jnp.float32).at[ids].add(grads.reshape(TOKENS, D))
    return (layer_out, table_grad)
```

```python
import functools

import jax
import jax.numpy as jnp
from jax import lax
from jax.experimental import pallas as pl
from jax.experimental.pallas import tpu as pltpu
from jax.sharding import PartitionSpec as P

HEADS = 4
EPS = 1e-05
PEERS = 8
PARTS = 2
F32 = jnp.float32
BF16 = jnp.bfloat16


def mul_nn(left, right):
    return lax.dot_general(left, right, (((1,), (0,)), ((), ())), preferred_element_type=F32)


def mul_nt(left, right):
    return lax.dot_general(left, right, (((1,), (1,)), ((), ())), preferred_element_type=F32)


def iota(shape, axis):
    return lax.broadcasted_iota(jnp.int32, shape, axis)


def kernel(
    ring,
    owner_ref,
    offset_ref,
    lengths_ref,
    table_hbm,
    w_in_hbm,
    w_out_hbm,
    up_hbm,
    layer_hbm,
    grad_hbm,
    id_near,
    id_all,
    slot_rows,
    table,
    w_in,
    w_out,
    up_all,
    w_head,
    rows_out,
    rows_z,
    rows_x,
    rows_in,
    emb_all,
    normed_bf,
    pre,
    act,
    kv_rows,
    weights,
    slopes,
    grad_gated,
    attended,
    sums,
    gated_out,
    gated_in,
    gp_out,
    gp_in,
    normed_t,
    up_t,
    g_out,
    g_z,
    g_x,
    g_in,
    layer_v,
    grad_v,
    local_sem,
    send_sem,
    recv_sem,
):
    tokens = 128
    width = table.shape[1]
    head = width // HEADS
    part = width // PARTS
    slots = 2 * PEERS * ring
    block = 2 * PEERS
    chunk_rows = 2 * ring
    me = lax.axis_index("table")
    seq = lax.axis_index("seq")
    z = me // PEERS
    p = me % PEERS

    def near(step):
        return (z * PEERS + (p + step) % PEERS, seq)

    def far(step):
        return (((z + step) % ring) * PEERS + p, seq)

    def beside(step):
        return (me, (seq + step) % HEADS)

    def send(src, dst, group, device):
        pltpu.make_async_remote_copy(
            src_ref=src,
            dst_ref=dst,
            send_sem=send_sem.at[group],
            recv_sem=recv_sem.at[group],
            device_id=device,
            device_id_type=pl.DeviceIdType.MESH,
        ).start()

    def await_bytes(view, sem):
        pltpu.make_async_copy(view, view, sem).wait()

    def rows(start, size):
        return pl.ds(pl.multiple_of(start, size), size)

    ID_NEAR, ID_FAR, UP, SLOTS, SUMS, GATED = range(6)
    GP = 6
    Z0 = 10
    X0 = Z0 + PARTS
    Y0 = X0 + PARTS
    GZ0 = Y0 + PARTS
    GX0 = GZ0 + PARTS
    GY0 = GX0 + PARTS

    up_copy = pltpu.make_async_copy(up_hbm, up_all.at[rows(seq * tokens, tokens), :], local_sem.at[0])
    up_copy.start()
    table_copy = pltpu.make_async_copy(table_hbm, table, local_sem.at[1])
    table_copy.start()
    in_copy = pltpu.make_async_copy(w_in_hbm, w_in, local_sem.at[2])
    in_copy.start()
    out_copy = pltpu.make_async_copy(w_out_hbm, w_out, local_sem.at[3])
    out_copy.start()

    owner = owner_ref[...]
    code = owner * table.shape[0] + offset_ref[...]
    id_near[p] = jnp.broadcast_to(code, (8, tokens))

    barrier = pltpu.get_barrier_semaphore()
    for step in range(1, PEERS):
        pl.semaphore_signal(barrier, inc=1, device_id=near(step), device_id_type=pl.DeviceIdType.MESH)
    for step in range(1, HEADS):
        pl.semaphore_signal(barrier, inc=1, device_id=beside(step), device_id_type=pl.DeviceIdType.MESH)

    @pl.loop(1, ring)
    def _(step):
        pl.semaphore_signal(barrier, inc=1, device_id=far(step), device_id_type=pl.DeviceIdType.MESH)

    pl.semaphore_wait(barrier, PEERS + ring + HEADS - 3)

    for step in range(1, PEERS):
        send(id_near.at[p], id_near.at[p], ID_NEAR, near(step))
    up_copy.wait()
    for step in range(1, HEADS):
        mine = up_all.at[rows(seq * tokens, tokens), :]
        send(mine, mine, UP, beside(step))

    owner_lane = jnp.broadcast_to(owner.astype(F32), (tokens, tokens))
    owner_sub = owner_lane.T
    n_sub = iota((tokens, tokens), 0)
    n_lane = iota((tokens, tokens), 1)
    same = owner_lane == owner_sub
    second_lane = jnp.max(jnp.where(same & (n_sub < n_lane), 1.0, 0.0), axis=0, keepdims=True)
    second_sub = jnp.max(jnp.where(same & (n_lane < n_sub), 1.0, 0.0), axis=1, keepdims=True)
    own_lane = owner
    slot_lane = (own_lane // PEERS) * block + second_lane.astype(jnp.int32) * PEERS + own_lane % PEERS
    own_sub = owner_sub[:, :1].astype(jnp.int32)
    slot_sub = (own_sub % PEERS) * chunk_rows + (own_sub // PEERS) * 2 + second_sub.astype(jnp.int32)
    pick_in = jnp.where(iota((tokens, slots), 1) == slot_sub, 1.0, 0.0).astype(BF16)
    place_out = jnp.where(iota((slots, tokens), 0) == slot_lane, 1.0, 0.0).astype(BF16)
    row_to = iota((slots, slots), 0)
    row_from = iota((slots, slots), 1)
    rest = row_to % chunk_rows
    source_row = (rest // 2) * block + (rest % 2) * PEERS + row_to // chunk_rows
    regroup = jnp.where(row_from == source_row, 1.0, 0.0).astype(BF16)

    await_bytes(id_near.at[pl.ds(0, PEERS - 1)], recv_sem.at[ID_NEAR])
    id_all[z] = jnp.concatenate([id_near[i, 0:1, :] for i in range(PEERS)], axis=0)

    @pl.loop(1, ring)
    def _(step):
        send(id_all.at[z], id_all.at[z], ID_FAR, far(step))

    in_copy.wait()
    for i in range(4):
        columns = pl.ds(pl.multiple_of(i * width + seq * head, head), head)
        w_head[i * head : (i + 1) * head, :] = w_in[:, columns].T
    table_copy.wait()
    out_copy.wait()

    await_bytes(id_all.at[pl.ds(0, ring - 1)], recv_sem.at[ID_FAR])
    codes = id_all[...].reshape(ring * PEERS, tokens)
    wanted = (codes // table.shape[0]) == me
    offsets = (codes % table.shape[0]).astype(F32)
    place = iota((ring * PEERS, tokens), 1).astype(F32)
    first = jnp.min(jnp.where(wanted, place, 1000.0), axis=1, keepdims=True)
    last = jnp.max(jnp.where(wanted, place, -1.0), axis=1, keepdims=True)
    first_off = jnp.sum(jnp.where(place == first, offsets, 0.0), axis=1, keepdims=True)
    last_off = jnp.sum(jnp.where(place == last, offsets, 0.0), axis=1, keepdims=True)
    none = float(table.shape[0])
    first_off = jnp.where(first < 1000.0, first_off, none)
    last_off = jnp.where(last > first, last_off, none)
    row_id = iota((ring * PEERS, table.shape[0]), 1).astype(F32)

    def interleave(one, two):
        both = [x.reshape(ring, PEERS, x.shape[1]) for x in (one, two)]
        return jnp.concatenate(both, axis=1).reshape(slots, one.shape[1])

    chosen = interleave(
        jnp.where(row_id == first_off, 1.0, 0.0), jnp.where(row_id == last_off, 1.0, 0.0)
    ).astype(BF16)
    for c in range(PARTS):
        rows_out[c] = mul_nn(chosen, table[:, c * part : (c + 1) * part]).astype(BF16)
        mine = rows(z * block, block)

        @pl.loop(1, ring)
        def _(step, c=c, mine=mine):
            there = rows(((z + step) % ring) * block, block)
            send(rows_out.at[c, there, :], rows_z.at[c, mine, :], Z0 + c, far(step))

        rows_z[c, mine, :] = rows_out[c, mine, :]

    slot_off = interleave(
        jnp.broadcast_to(first_off, (ring * PEERS, tokens)),
        jnp.broadcast_to(last_off, (ring * PEERS, tokens)),
    ).T[:8]
    high = jnp.floor(slot_off * 0.0625)
    digits = jnp.concatenate([high, slot_off - 16.0 * high], axis=0).astype(BF16)
    moved = mul_nt(digits, regroup)
    slot_rows[seq] = moved[:8] * 16.0 + moved[8:]
    for step in range(1, HEADS):
        send(slot_rows.at[seq], slot_rows.at[seq], SLOTS, beside(step))

    await_bytes(up_all.at[pl.ds(0, 3 * tokens), :], recv_sem.at[UP])
    grad_gated[...] = mul_nt(w_out[rows(seq * head, head), :], up_all[...])
    up_t[...] = up_all[rows(seq * tokens, tokens), :].astype(F32).T

    def pass_near(c, src, src_sem, mid, dst, base, sem):
        await_bytes(src.at[c, pl.ds(0, slots - block), :], recv_sem.at[src_sem + c])
        mid[c] = mul_nn(regroup, src[c]).astype(BF16)
        mine = rows(base + p * chunk_rows, chunk_rows)
        for step in range(1, PEERS):
            there = rows(((p + step) % PEERS) * chunk_rows, chunk_rows)
            send(mid.at[c, there, :], dst.at[c, mine, :], sem + c, near(step))
        dst[c, mine, :] = mid[c, rows(p * chunk_rows, chunk_rows), :]

    def gather_rows(c):
        await_bytes(rows_in.at[c, pl.ds(0, slots - chunk_rows), :], recv_sem.at[X0 + c])
        mine = rows(seq * tokens, tokens)
        emb_all[c, mine, :] = mul_nn(pick_in, rows_in[c]).astype(BF16)
        for step in range(1, HEADS):
            send(emb_all.at[c, mine, :], emb_all.at[c, mine, :], Y0 + c, beside(step))

    for c in range(PARTS):
        pass_near(c, rows_z, Z0, rows_x, rows_in, 0, X0)
        if c > 0:
            gather_rows(c - 1)
    gather_rows(PARTS - 1)

    own = rows(seq * tokens, tokens)
    emb_own = jnp.concatenate([emb_all[c, own, :] for c in range(PARTS)], axis=1).astype(F32)
    emb_t = emb_own.T
    centered_t = emb_t - jnp.mean(emb_t, axis=0, keepdims=True)
    inv_own = lax.rsqrt(jnp.mean(centered_t * centered_t, axis=0, keepdims=True) + EPS)
    normed_t[...] = centered_t * inv_own

    for c in range(PARTS):
        await_bytes(emb_all.at[c, pl.ds(0, 3 * tokens), :], recv_sem.at[Y0 + c])
    for i in range(HEADS):
        here = slice(i * tokens, (i + 1) * tokens)
        wide = jnp.concatenate([emb_all[c, here, :] for c in range(PARTS)], axis=1).astype(F32)
        centered = wide - jnp.mean(wide, axis=1, keepdims=True)
        inv = lax.rsqrt(jnp.mean(centered * centered, axis=1, keepdims=True) + EPS)
        normed_bf[here, :] = (centered * inv).astype(BF16)

    pre[...] = mul_nt(w_head[...], normed_bf[...])
    for i in range(4):
        here = slice(i * head, (i + 1) * head)
        x = pre[here, :]
        act[here, :] = (x * jax.nn.sigmoid(x)).astype(BF16)
    gate = slice(0, head)
    value = slice(head, 2 * head)
    query = slice(2 * head, 3 * head)
    key = slice(3 * head, 4 * head)
    kv_rows[0] = act[value, :].T
    kv_rows[1] = act[key, :].T

    start_two = lengths_ref[0, 0]
    start_three = start_two + lengths_ref[0, 1]

    def user_of(position):
        return (position >= start_two).astype(jnp.int32) + (position >= start_three).astype(jnp.int32)

    scale = head ** (-0.5)
    blocks = [slice(i * tokens, (i + 1) * tokens) for i in range(HEADS)]

    def keys_of(j):
        return slice(max(0, j - 2) * tokens, (j + 1) * tokens)

    def queries_of(i):
        return slice(i * tokens, min(HEADS, i + 3) * tokens)

    for j in range(HEADS):
        here, ms = blocks[j], keys_of(j)
        count = ms.stop - ms.start
        scores = mul_nn(kv_rows[1, ms, :], act[query, here]) * scale
        m_at = iota((count, 1), 0) + ms.start
        n_at = iota((1, tokens), 1) + here.start
        allowed = (user_of(m_at) == user_of(n_at)) & (m_at <= n_at)
        logistic = jax.nn.sigmoid(scores)
        weight = jnp.where(allowed, scores * logistic, 0.0).astype(BF16)
        weights[ms, here] = weight
        slopes[ms, here] = jnp.where(
            allowed, logistic * (1.0 + scores * (1.0 - logistic)) * scale, 0.0
        )
        out = mul_nn(act[value, ms], weight)
        attended[:, here] = out
        g = grad_gated[:, here] * act[gate, here].astype(F32)
        out_mean = jnp.mean(out, axis=0, keepdims=True)
        g_mean = jnp.mean(g, axis=0, keepdims=True)
        out_c = out - out_mean
        out_sq = jnp.sum(out_c * out_c, axis=0, keepdims=True)
        cross = jnp.sum(out_c * (g - g_mean), axis=0, keepdims=True)
        sums[seq, :, here] = jnp.concatenate(
            [out_mean, out_sq, g_mean, cross, jnp.zeros((4, tokens), F32)], axis=0
        )
    for step in range(1, HEADS):
        send(sums.at[seq], sums.at[seq], SUMS, beside(step))

    await_bytes(sums.at[pl.ds(0, HEADS - 1)], recv_sem.at[SUMS])
    parts = [sums[i] for i in range(HEADS)]
    means = [s[0:1] for s in parts]
    g_means = [s[2:3] for s in parts]
    out_mean = sum(means) * (1.0 / HEADS)
    g_mean = sum(g_means) * (1.0 / HEADS)
    out_sq = sum(s[1:2] for s in parts) + head * sum((m - out_mean) * (m - out_mean) for m in means)
    cross = sum(s[3:4] for s in parts) + head * sum(
        (m - out_mean) * (g - g_mean) for m, g in zip(means, g_means)
    )
    inv_out = lax.rsqrt(out_sq * (1.0 / width) + EPS)
    slant = inv_out * cross * (1.0 / width)

    def pre_slope(part_of, here):
        x = pre[part_of, here]
        logistic = jax.nn.sigmoid(x)
        return logistic * (1.0 + x * (1.0 - logistic))

    def exchange(i):
        here = pl.ds(i * head, head)
        mine = pl.ds(pl.multiple_of(i * width + seq * head, head), head)
        for step in range(1, HEADS):
            there = (seq + step) % HEADS
            send(gp_out.at[there, here, :], gp_in.at[mine, :], GP + i, beside(step))
        gp_in[mine, :] = gp_out[seq, here, :]

    grad_out = []
    for j in range(HEADS):
        here = blocks[j]
        gate_u = act[gate, here].astype(F32)
        raw = grad_gated[:, here]
        normed = (attended[:, here] - out_mean[:, here]) * inv_out[:, here]
        gated_out[j] = (normed * gate_u).astype(BF16)
        gp_out[j, gate, :] = (raw * normed * pre_slope(gate, here)).astype(BF16)
        grad_out.append(
            (
                inv_out[:, here]
                * (raw * gate_u - g_mean[:, here] - normed * slant[:, here])
            ).astype(BF16)
        )
    exchange(0)
    mine = rows(seq * head, head)
    for step in range(1, HEADS):
        send(gated_out.at[(seq + step) % HEADS], gated_in.at[mine, :], GATED, beside(step))
    gated_in[mine, :] = gated_out[seq]
    grad_out = jnp.concatenate(grad_out, axis=1)
    for i in range(HEADS):
        ns = queries_of(i)
        found = mul_nt(grad_out[:, ns], weights[blocks[i], ns])
        gp_out[i, value, :] = (found * pre_slope(value, blocks[i])).astype(BF16)
    exchange(1)
    grad_score = {}
    for j in range(HEADS):
        ms = keys_of(j)
        moved = mul_nn(kv_rows[0, ms, :], grad_out[:, blocks[j]])
        moved = (moved * slopes[ms, blocks[j]]).astype(BF16)
        grad_score[j] = moved
        weights[ms, blocks[j]] = moved
        found = mul_nn(act[key, ms], moved)
        gp_out[j, query, :] = (found * pre_slope(query, blocks[j])).astype(BF16)
    exchange(2)
    for i in range(HEADS):
        ns = queries_of(i)
        found = mul_nt(act[query, ns], weights[blocks[i], ns])
        gp_out[i, key, :] = (found * pre_slope(key, blocks[i])).astype(BF16)
    exchange(3)

    grad_normed = jnp.zeros((width, tokens), F32)
    for i in range(4):
        await_bytes(gp_in.at[pl.ds(i * width, 3 * head), :], recv_sem.at[GP + i])
        here = slice(i * width, (i + 1) * width)
        grad_normed = grad_normed + mul_nn(w_in[:, here], gp_in[here, :])
    normed = normed_t[...]
    grad_rows = up_t[...] + inv_own * (
        grad_normed
        - jnp.mean(grad_normed, axis=0, keepdims=True)
        - normed * jnp.mean(grad_normed * normed, axis=0, keepdims=True)
    )
    grad_rows = grad_rows.astype(BF16)
    for c in range(PARTS):
        g_out[c] = mul_nt(place_out, grad_rows[c * part : (c + 1) * part]).astype(BF16)
        mine = rows(z * block, block)

        @pl.loop(1, ring)
        def _(step, c=c, mine=mine):
            there = rows(((z + step) % ring) * block, block)
            send(g_out.at[c, there, :], g_z.at[c, mine, :], GZ0 + c, far(step))

        g_z[c, mine, :] = g_out[c, mine, :]

    await_bytes(gated_in.at[pl.ds(0, 3 * head), :], recv_sem.at[GATED])
    layer_v[...] = (emb_own + mul_nn(gated_in[...].T, w_out[...])).astype(BF16)
    layer_copy = pltpu.make_async_copy(layer_v, layer_hbm, local_sem.at[4])
    layer_copy.start()

    await_bytes(slot_rows.at[pl.ds(0, HEADS - 1)], recv_sem.at[SLOTS])
    table_row = iota((table.shape[0], slots), 0).astype(F32)
    spread = jnp.concatenate(
        [
            jnp.where(table_row == slot_rows[i, 0:1, :], 1.0, 0.0).astype(BF16)
            for i in range(HEADS)
        ],
        axis=1,
    )

    def pass_beside(c):
        mine = rows(seq * slots, slots)
        await_bytes(g_in.at[c, pl.ds(0, slots - chunk_rows), :], recv_sem.at[GX0 + c])
        for step in range(1, HEADS):
            send(g_in.at[c, mine, :], g_in.at[c, mine, :], GY0 + c, beside(step))

    for c in range(PARTS):
        pass_near(c, g_z, GZ0, g_x, g_in, seq * slots, GX0)
        if c > 0:
            pass_beside(c - 1)
    pass_beside(PARTS - 1)
    grad_copies = []
    for c in range(PARTS):
        await_bytes(g_in.at[c, pl.ds(0, 3 * slots), :], recv_sem.at[GY0 + c])
        grad_v[c] = mul_nn(spread, g_in[c])
        copy = pltpu.make_async_copy(
            grad_v.at[c], grad_hbm.at[:, pl.ds(c * part, part)], local_sem.at[5 + c]
        )
        copy.start()
        grad_copies.append(copy)

    await_bytes(id_near.at[pl.ds(0, PEERS - 1)], send_sem.at[ID_NEAR])
    await_bytes(id_all.at[pl.ds(0, ring - 1)], send_sem.at[ID_FAR])
    await_bytes(up_all.at[pl.ds(0, 3 * tokens), :], send_sem.at[UP])
    await_bytes(slot_rows.at[pl.ds(0, HEADS - 1)], send_sem.at[SLOTS])
    await_bytes(sums.at[pl.ds(0, HEADS - 1)], send_sem.at[SUMS])
    await_bytes(gated_in.at[pl.ds(0, 3 * head), :], send_sem.at[GATED])
    for i in range(4):
        await_bytes(gp_in.at[pl.ds(i * width, 3 * head), :], send_sem.at[GP + i])
    for c in range(PARTS):
        await_bytes(rows_z.at[c, pl.ds(0, slots - block), :], send_sem.at[Z0 + c])
        await_bytes(rows_in.at[c, pl.ds(0, slots - chunk_rows), :], send_sem.at[X0 + c])
        await_bytes(emb_all.at[c, pl.ds(0, 3 * tokens), :], send_sem.at[Y0 + c])
        await_bytes(g_z.at[c, pl.ds(0, slots - block), :], send_sem.at[GZ0 + c])
        await_bytes(g_in.at[c, pl.ds(0, slots - chunk_rows), :], send_sem.at[GX0 + c])
        await_bytes(g_in.at[c, pl.ds(0, 3 * slots), :], send_sem.at[GY0 + c])
    layer_copy.wait()
    for copy in grad_copies:
        copy.wait()


def local(embedding_table, project_in, project_out, row_owner, row_offset, user_lengths, upstream):
    tokens = row_offset.shape[0]
    table_rows, width = embedding_table.shape
    ring = lax.axis_size("table") // PEERS
    group = tokens * HEADS
    slots = 2 * PEERS * ring
    part = width // PARTS
    head = width // HEADS
    any_spec = pl.BlockSpec(memory_space=pl.ANY)
    vmem_spec = pl.BlockSpec(memory_space=pltpu.VMEM)
    smem_spec = pl.BlockSpec(memory_space=pltpu.SMEM)
    vmem = pltpu.VMEM
    return pl.pallas_call(
        functools.partial(kernel, ring),
        out_shape=(
            jax.ShapeDtypeStruct((tokens, width), BF16),
            jax.ShapeDtypeStruct((table_rows, width), F32),
        ),
        in_specs=[vmem_spec, vmem_spec, smem_spec] + [any_spec] * 4,
        out_specs=(any_spec, any_spec),
        scratch_shapes=[
            vmem((PEERS, 8, tokens), jnp.int32),
            vmem((ring, PEERS, tokens), jnp.int32),
            vmem((HEADS, 8, slots), F32),
            vmem((table_rows, width), BF16),
            vmem((width, 4 * width), BF16),
            vmem((width, width), BF16),
            vmem((group, width), BF16),
            vmem((4 * head, width), BF16),
            vmem((PARTS, slots, part), BF16),
            vmem((PARTS, slots, part), BF16),
            vmem((PARTS, slots, part), BF16),
            vmem((PARTS, slots, part), BF16),
            vmem((PARTS, group, part), BF16),
            vmem((group, width), BF16),
            vmem((4 * head, group), F32),
            vmem((4 * head, group), BF16),
            vmem((2, group, head), BF16),
            vmem((group, group), BF16),
            vmem((group, group), F32),
            vmem((head, group), F32),
            vmem((head, group), F32),
            vmem((HEADS, 8, group), F32),
            vmem((HEADS, head, tokens), BF16),
            vmem((width, tokens), BF16),
            vmem((HEADS, 4 * head, tokens), BF16),
            vmem((4 * width, tokens), BF16),
            vmem((width, tokens), F32),
            vmem((width, tokens), F32),
            vmem((PARTS, slots, part), BF16),
            vmem((PARTS, slots, part), BF16),
            vmem((PARTS, slots, part), BF16),
            vmem((PARTS, HEADS * slots, part), BF16),
            vmem((tokens, width), BF16),
            vmem((PARTS, table_rows, part), F32),
            pltpu.SemaphoreType.DMA((5 + PARTS,)),
            pltpu.SemaphoreType.DMA((10 + 6 * PARTS,)),
            pltpu.SemaphoreType.DMA((10 + 6 * PARTS,)),
        ],
        compiler_params=pltpu.CompilerParams(
            collective_id=0, has_side_effects=True, vmem_limit_bytes=48 * 2**20
        ),
        name="hstu_step",
    )(
        row_owner.reshape(1, tokens),
        row_offset.reshape(1, tokens),
        user_lengths,
        embedding_table,
        project_in,
        project_out,
        upstream,
    )


def solution(mesh):
    return jax.shard_map(
        local,
        mesh=mesh,
        in_specs=(
            P("table", None),
            P(),
            P(),
            P(("table", "seq"), None),
            P(("table", "seq")),
            P("table", None),
            P(("table", "seq"), None),
        ),
        out_specs=(P(("table", "seq"), None), P("table", None)),
        check_vma=False,
    )
```

```python
import functools

import jax
import jax.numpy as jnp
from jax import lax
from jax.experimental import pallas as pl
from jax.experimental.pallas import tpu as pltpu
from jax.sharding import PartitionSpec as P

HEADS = 4
EPS = 1e-05
PEERS = 8
PARTS = 2
F32 = jnp.float32
BF16 = jnp.bfloat16


def mul_nn(left, right):
    return lax.dot_general(left, right, (((1,), (0,)), ((), ())), preferred_element_type=F32)


def mul_nt(left, right):
    return lax.dot_general(left, right, (((1,), (1,)), ((), ())), preferred_element_type=F32)


def iota(shape, axis):
    return lax.broadcasted_iota(jnp.int32, shape, axis)


def kernel(
    ring,
    owner_hbm,
    offset_hbm,
    lengths_hbm,
    table_hbm,
    w_in_hbm,
    w_out_hbm,
    up_hbm,
    layer_ref,
    grad_ref,
    owner_v,
    offset_v,
    lengths,
    id_near,
    id_all,
    slot_rows,
    table,
    w_in,
    w_out,
    up_all,
    w_head,
    rows_out,
    rows_z,
    rows_x,
    rows_in,
    emb_all,
    normed_bf,
    pre,
    act,
    kv_rows,
    weights,
    slopes,
    grad_gated,
    attended,
    sums,
    gated_out,
    gated_in,
    gp_out,
    gp_in,
    normed_t,
    up_t,
    g_out,
    g_z,
    g_x,
    g_in,
    local_sem,
    send_sem,
    recv_sem,
):
    tokens = 128
    width = table.shape[1]
    head = width // HEADS
    part = width // PARTS
    slots = 2 * PEERS * ring
    block = 2 * PEERS
    chunk_rows = 2 * ring
    me = lax.axis_index("table")
    seq = lax.axis_index("seq")
    z = me // PEERS
    p = me % PEERS

    chip = p // 2
    core = p % 2

    def near_index(step):
        over, flip = ((1, 0), (3, 0), (1, 1), (3, 1), (2, 0), (2, 1), (0, 1))[step]
        return ((chip + over) % (PEERS // 2)) * 2 + (core + flip) % 2

    def near(step):
        return (z * PEERS + near_index(step), seq)

    def turn(i):
        hops = (ring - i) // 2
        odd = i % 2
        return z + odd * hops + (1 - odd) * (ring - hops)

    def far_index(i):
        return turn(i) % ring

    def far(i):
        return (far_index(i) * PEERS + p, seq)

    def beside_index(step):
        return (seq + (1, 3, 2)[step]) % HEADS

    def beside(step):
        return (me, beside_index(step))

    leaving = []

    def send(src, dst, group, device):
        pltpu.make_async_remote_copy(
            src_ref=src,
            dst_ref=dst,
            send_sem=send_sem.at[group],
            recv_sem=recv_sem.at[group],
            device_id=device,
            device_id_type=pl.DeviceIdType.MESH,
        ).start()

    def await_bytes(view, sem):
        pltpu.make_async_copy(view, view, sem).wait()

    def rows(start, size):
        return pl.ds(pl.multiple_of(start, size), size)

    ID_NEAR, ID_FAR, SLOTS, SUMS, GATED = range(5)
    GP = 5
    UP = 9
    Z0 = 12
    X0 = Z0 + PARTS
    GZ0 = X0 + PARTS
    GX0 = GZ0 + PARTS
    Y0 = GX0 + PARTS
    GY0 = Y0 + 3 * PARTS

    def spread(buf, start, size, group):
        mine = rows(start + seq * size, size)
        for way in (0, 1):
            send(buf.at[mine, :], buf.at[mine, :], group + way, beside(way))
            leaving.append((group + way, buf.at[pl.ds(start, size), :]))

    def relay(buf, start, size, group):
        half = size // 2
        for way in (0, 1):
            await_bytes(buf.at[pl.ds(start, size), :], recv_sem.at[group + way])
            block_of = beside_index(1 - way)
            here = rows(start + block_of * size + way * half, half)
            send(buf.at[here, :], buf.at[here, :], group + 2, beside(way))
        leaving.append((group + 2, buf.at[pl.ds(start, size), :]))

    def settle(buf, start, size, group):
        await_bytes(buf.at[pl.ds(start, size), :], recv_sem.at[group + 2])

    owner_copy = pltpu.make_async_copy(owner_hbm, owner_v, local_sem.at[4])
    owner_copy.start()
    offset_copy = pltpu.make_async_copy(offset_hbm, offset_v, local_sem.at[5])
    offset_copy.start()
    lengths_copy = pltpu.make_async_copy(lengths_hbm, lengths, local_sem.at[6])
    lengths_copy.start()
    up_copy = pltpu.make_async_copy(up_hbm, up_all.at[rows(seq * tokens, tokens), :], local_sem.at[0])
    up_copy.start()
    table_copy = pltpu.make_async_copy(table_hbm, table, local_sem.at[1])
    table_copy.start()
    in_copy = pltpu.make_async_copy(w_in_hbm, w_in, local_sem.at[2])
    in_copy.start()
    out_copy = pltpu.make_async_copy(w_out_hbm, w_out, local_sem.at[3])
    out_copy.start()

    barrier = pltpu.get_barrier_semaphore()
    for step in range(PEERS - 1):
        pl.semaphore_signal(barrier, inc=1, device_id=near(step), device_id_type=pl.DeviceIdType.MESH)
    for step in range(HEADS - 1):
        pl.semaphore_signal(barrier, inc=1, device_id=beside(step), device_id_type=pl.DeviceIdType.MESH)

    @pl.loop(0, ring - 1)
    def _(step):
        pl.semaphore_signal(barrier, inc=1, device_id=far(step), device_id_type=pl.DeviceIdType.MESH)

    owner_copy.wait()
    offset_copy.wait()
    owner = owner_v[...]
    code = owner * table.shape[0] + offset_v[...]
    id_near[p] = jnp.broadcast_to(code, (8, tokens))
    pl.semaphore_wait(barrier, PEERS + ring + HEADS - 3)

    for step in range(PEERS - 1):
        send(id_near.at[p], id_near.at[p], ID_NEAR, near(step))
    leaving.append((ID_NEAR, id_near.at[pl.ds(0, PEERS - 1)]))
    up_copy.wait()
    spread(up_all, 0, tokens, UP)

    owner_lane = jnp.broadcast_to(owner.astype(F32), (tokens, tokens))
    owner_sub = owner_lane.T
    n_sub = iota((tokens, tokens), 0)
    n_lane = iota((tokens, tokens), 1)
    same = owner_lane == owner_sub
    second_lane = jnp.max(jnp.where(same & (n_sub < n_lane), 1.0, 0.0), axis=0, keepdims=True)
    second_sub = jnp.max(jnp.where(same & (n_lane < n_sub), 1.0, 0.0), axis=1, keepdims=True)
    own_lane = owner
    slot_lane = (own_lane // PEERS) * block + second_lane.astype(jnp.int32) * PEERS + own_lane % PEERS
    own_sub = owner_sub[:, :1].astype(jnp.int32)
    slot_sub = (own_sub % PEERS) * chunk_rows + (own_sub // PEERS) * 2 + second_sub.astype(jnp.int32)
    pick_in = jnp.where(iota((tokens, slots), 1) == slot_sub, 1.0, 0.0).astype(BF16)
    place_out = jnp.where(iota((slots, tokens), 0) == slot_lane, 1.0, 0.0).astype(BF16)
    row_to = iota((slots, slots), 0)
    row_from = iota((slots, slots), 1)
    rest = row_to % chunk_rows
    source_row = (rest // 2) * block + (rest % 2) * PEERS + row_to // chunk_rows
    regroup = jnp.where(row_from == source_row, 1.0, 0.0).astype(BF16)

    await_bytes(id_near.at[pl.ds(0, PEERS - 1)], recv_sem.at[ID_NEAR])
    id_all[z] = jnp.concatenate([id_near[i, 0:1, :] for i in range(PEERS)], axis=0)

    @pl.loop(0, ring - 1)
    def _(step):
        send(id_all.at[z], id_all.at[z], ID_FAR, far(step))

    leaving.append((ID_FAR, id_all.at[pl.ds(0, ring - 1)]))

    in_copy.wait()
    for i in range(4):
        columns = pl.ds(pl.multiple_of(i * width + seq * head, head), head)
        w_head[i * head : (i + 1) * head, :] = w_in[:, columns].T
    table_copy.wait()
    out_copy.wait()

    await_bytes(id_all.at[pl.ds(0, ring - 1)], recv_sem.at[ID_FAR])
    codes = id_all[...].reshape(ring * PEERS, tokens)
    wanted = (codes // table.shape[0]) == me
    offsets = (codes % table.shape[0]).astype(F32)
    place = iota((ring * PEERS, tokens), 1).astype(F32)
    first = jnp.min(jnp.where(wanted, place, 1000.0), axis=1, keepdims=True)
    last = jnp.max(jnp.where(wanted, place, -1.0), axis=1, keepdims=True)
    first_off = jnp.sum(jnp.where(place == first, offsets, 0.0), axis=1, keepdims=True)
    last_off = jnp.sum(jnp.where(place == last, offsets, 0.0), axis=1, keepdims=True)
    none = float(table.shape[0])
    first_off = jnp.where(first < 1000.0, first_off, none)
    last_off = jnp.where(last > first, last_off, none)
    row_id = iota((ring * PEERS, table.shape[0]), 1).astype(F32)

    def interleave(one, two):
        both = [x.reshape(ring, PEERS, x.shape[1]) for x in (one, two)]
        return jnp.concatenate(both, axis=1).reshape(slots, one.shape[1])

    chosen = interleave(
        jnp.where(row_id == first_off, 1.0, 0.0), jnp.where(row_id == last_off, 1.0, 0.0)
    ).astype(BF16)
    for c in range(PARTS):
        rows_out[c] = mul_nn(chosen, table[:, c * part : (c + 1) * part]).astype(BF16)
        mine = rows(z * block, block)

        @pl.loop(0, ring - 1)
        def _(step, c=c, mine=mine):
            there = rows(far_index(step) * block, block)
            send(rows_out.at[c, there, :], rows_z.at[c, mine, :], Z0 + c, far(step))

        leaving.append((Z0 + c, rows_z.at[c, pl.ds(0, slots - block), :]))

        rows_z[c, mine, :] = rows_out[c, mine, :]

    slot_off = interleave(
        jnp.broadcast_to(first_off, (ring * PEERS, tokens)),
        jnp.broadcast_to(last_off, (ring * PEERS, tokens)),
    ).T[:8]
    high = jnp.floor(slot_off * 0.0625)
    digits = jnp.concatenate([high, slot_off - 16.0 * high], axis=0).astype(BF16)
    moved = mul_nt(digits, regroup)
    slot_rows[seq] = moved[:8] * 16.0 + moved[8:]
    for step in range(HEADS - 1):
        send(slot_rows.at[seq], slot_rows.at[seq], SLOTS, beside(step))
    leaving.append((SLOTS, slot_rows.at[pl.ds(0, HEADS - 1)]))

    relay(up_all, 0, tokens, UP)
    settle(up_all, 0, tokens, UP)
    grad_gated[...] = mul_nt(w_out[rows(seq * head, head), :], up_all[...])
    up_t[...] = up_all[rows(seq * tokens, tokens), :].astype(F32).T

    def pass_near(c, src, src_sem, mid, dst, base, sem):
        await_bytes(src.at[c, pl.ds(0, slots - block), :], recv_sem.at[src_sem + c])
        mid[c] = mul_nn(regroup, src[c]).astype(BF16)
        mine = rows(base + p * chunk_rows, chunk_rows)
        for step in range(PEERS - 1):
            there = rows(near_index(step) * chunk_rows, chunk_rows)
            send(mid.at[c, there, :], dst.at[c, mine, :], sem + c, near(step))
        leaving.append((sem + c, dst.at[c, pl.ds(0, slots - chunk_rows), :]))
        dst[c, mine, :] = mid[c, rows(p * chunk_rows, chunk_rows), :]

    def gather_rows(c):
        await_bytes(rows_in.at[c, pl.ds(0, slots - chunk_rows), :], recv_sem.at[X0 + c])
        mine = rows(seq * tokens, tokens)
        emb_all[c, mine, :] = mul_nn(pick_in, rows_in[c]).astype(BF16)
        spread(emb_all.at[c], 0, tokens, Y0 + 3 * c)

    for c in range(PARTS):
        pass_near(c, rows_z, Z0, rows_x, rows_in, 0, X0)
        if c > 0:
            gather_rows(c - 1)
        if c > 1:
            relay(emb_all.at[c - 2], 0, tokens, Y0 + 3 * (c - 2))
    gather_rows(PARTS - 1)
    for c in range(max(0, PARTS - 2), PARTS):
        relay(emb_all.at[c], 0, tokens, Y0 + 3 * c)

    own = rows(seq * tokens, tokens)
    emb_own = jnp.concatenate([emb_all[c, own, :] for c in range(PARTS)], axis=1).astype(F32)
    emb_t = emb_own.T
    centered_t = emb_t - jnp.mean(emb_t, axis=0, keepdims=True)
    inv_own = lax.rsqrt(jnp.mean(centered_t * centered_t, axis=0, keepdims=True) + EPS)
    normed_t[...] = centered_t * inv_own

    for c in range(PARTS):
        settle(emb_all.at[c], 0, tokens, Y0 + 3 * c)
    for i in range(HEADS):
        here = slice(i * tokens, (i + 1) * tokens)
        wide = jnp.concatenate([emb_all[c, here, :] for c in range(PARTS)], axis=1).astype(F32)
        centered = wide - jnp.mean(wide, axis=1, keepdims=True)
        inv = lax.rsqrt(jnp.mean(centered * centered, axis=1, keepdims=True) + EPS)
        normed_bf[here, :] = (centered * inv).astype(BF16)

    pre[...] = mul_nt(w_head[...], normed_bf[...])
    for i in range(4):
        here = slice(i * head, (i + 1) * head)
        x = pre[here, :]
        act[here, :] = (x * jax.nn.sigmoid(x)).astype(BF16)
    gate = slice(0, head)
    value = slice(head, 2 * head)
    query = slice(2 * head, 3 * head)
    key = slice(3 * head, 4 * head)
    kv_rows[0] = act[value, :].T
    kv_rows[1] = act[key, :].T

    lengths_copy.wait()
    start_two = lengths[0, 0]
    start_three = start_two + lengths[0, 1]

    def user_of(position):
        return (position >= start_two).astype(jnp.int32) + (position >= start_three).astype(jnp.int32)

    scale = head ** (-0.5)
    blocks = [slice(i * tokens, (i + 1) * tokens) for i in range(HEADS)]

    def keys_of(j):
        return slice(max(0, j - 2) * tokens, (j + 1) * tokens)

    def queries_of(i):
        return slice(i * tokens, min(HEADS, i + 3) * tokens)

    for j in range(HEADS):
        here, ms = blocks[j], keys_of(j)
        count = ms.stop - ms.start
        scores = mul_nn(kv_rows[1, ms, :], act[query, here]) * scale
        m_at = iota((count, 1), 0) + ms.start
        n_at = iota((1, tokens), 1) + here.start
        allowed = (user_of(m_at) == user_of(n_at)) & (m_at <= n_at)
        logistic = jax.nn.sigmoid(scores)
        weight = jnp.where(allowed, scores * logistic, 0.0).astype(BF16)
        weights[ms, here] = weight
        slopes[ms, here] = jnp.where(
            allowed, logistic * (1.0 + scores * (1.0 - logistic)) * scale, 0.0
        )
        out = mul_nn(act[value, ms], weight)
        attended[:, here] = out
        g = grad_gated[:, here] * act[gate, here].astype(F32)
        out_mean = jnp.mean(out, axis=0, keepdims=True)
        g_mean = jnp.mean(g, axis=0, keepdims=True)
        out_c = out - out_mean
        out_sq = jnp.sum(out_c * out_c, axis=0, keepdims=True)
        cross = jnp.sum(out_c * (g - g_mean), axis=0, keepdims=True)
        sums[seq, :, here] = jnp.concatenate(
            [out_mean, out_sq, g_mean, cross, jnp.zeros((4, tokens), F32)], axis=0
        )
    for step in range(HEADS - 1):
        send(sums.at[seq], sums.at[seq], SUMS, beside(step))
    leaving.append((SUMS, sums.at[pl.ds(0, HEADS - 1)]))

    await_bytes(sums.at[pl.ds(0, HEADS - 1)], recv_sem.at[SUMS])
    parts = [sums[i] for i in range(HEADS)]
    means = [s[0:1] for s in parts]
    g_means = [s[2:3] for s in parts]
    out_mean = sum(means) * (1.0 / HEADS)
    g_mean = sum(g_means) * (1.0 / HEADS)
    out_sq = sum(s[1:2] for s in parts) + head * sum((m - out_mean) * (m - out_mean) for m in means)
    cross = sum(s[3:4] for s in parts) + head * sum(
        (m - out_mean) * (g - g_mean) for m, g in zip(means, g_means)
    )
    inv_out = lax.rsqrt(out_sq * (1.0 / width) + EPS)
    slant = inv_out * cross * (1.0 / width)

    def pre_slope(part_of, here):
        x = pre[part_of, here]
        logistic = jax.nn.sigmoid(x)
        return logistic * (1.0 + x * (1.0 - logistic))

    def exchange(i):
        here = pl.ds(i * head, head)
        mine = pl.ds(pl.multiple_of(i * width + seq * head, head), head)
        for step in range(HEADS - 1):
            there = beside_index(step)
            send(gp_out.at[there, here, :], gp_in.at[mine, :], GP + i, beside(step))
        leaving.append((GP + i, gp_in.at[pl.ds(i * width, 3 * head), :]))
        gp_in[mine, :] = gp_out[seq, here, :]

    grad_out = []
    for j in range(HEADS):
        here = blocks[j]
        gate_u = act[gate, here].astype(F32)
        raw = grad_gated[:, here]
        normed = (attended[:, here] - out_mean[:, here]) * inv_out[:, here]
        gated_out[j] = (normed * gate_u).astype(BF16)
        gp_out[j, gate, :] = (raw * normed * pre_slope(gate, here)).astype(BF16)
        grad_out.append(
            (
                inv_out[:, here]
                * (raw * gate_u - g_mean[:, here] - normed * slant[:, here])
            ).astype(BF16)
        )
    exchange(0)
    mine = rows(seq * head, head)
    for step in range(HEADS - 1):
        send(gated_out.at[beside_index(step)], gated_in.at[mine, :], GATED, beside(step))
    leaving.append((GATED, gated_in.at[pl.ds(0, 3 * head), :]))
    gated_in[mine, :] = gated_out[seq]
    grad_out = jnp.concatenate(grad_out, axis=1)
    for i in range(HEADS):
        ns = queries_of(i)
        found = mul_nt(grad_out[:, ns], weights[blocks[i], ns])
        gp_out[i, value, :] = (found * pre_slope(value, blocks[i])).astype(BF16)
    exchange(1)
    grad_score = {}
    for j in range(HEADS):
        ms = keys_of(j)
        moved = mul_nn(kv_rows[0, ms, :], grad_out[:, blocks[j]])
        moved = (moved * slopes[ms, blocks[j]]).astype(BF16)
        grad_score[j] = moved
        weights[ms, blocks[j]] = moved
        found = mul_nn(act[key, ms], moved)
        gp_out[j, query, :] = (found * pre_slope(query, blocks[j])).astype(BF16)
    exchange(2)
    for i in range(HEADS):
        ns = queries_of(i)
        found = mul_nt(act[query, ns], weights[blocks[i], ns])
        gp_out[i, key, :] = (found * pre_slope(key, blocks[i])).astype(BF16)
    exchange(3)

    grad_normed = jnp.zeros((width, tokens), F32)
    for i in range(4):
        await_bytes(gp_in.at[pl.ds(i * width, 3 * head), :], recv_sem.at[GP + i])
        here = slice(i * width, (i + 1) * width)
        grad_normed = grad_normed + mul_nn(w_in[:, here], gp_in[here, :])
    normed = normed_t[...]
    grad_rows = up_t[...] + inv_own * (
        grad_normed
        - jnp.mean(grad_normed, axis=0, keepdims=True)
        - normed * jnp.mean(grad_normed * normed, axis=0, keepdims=True)
    )
    grad_rows = grad_rows.astype(BF16)
    for c in range(PARTS):
        g_out[c] = mul_nt(place_out, grad_rows[c * part : (c + 1) * part]).astype(BF16)
        mine = rows(z * block, block)

        @pl.loop(0, ring - 1)
        def _(step, c=c, mine=mine):
            there = rows(far_index(step) * block, block)
            send(g_out.at[c, there, :], g_z.at[c, mine, :], GZ0 + c, far(step))

        leaving.append((GZ0 + c, g_z.at[c, pl.ds(0, slots - block), :]))

        g_z[c, mine, :] = g_out[c, mine, :]

    await_bytes(gated_in.at[pl.ds(0, 3 * head), :], recv_sem.at[GATED])
    layer_ref[...] = (emb_own + mul_nn(gated_in[...].T, w_out[...])).astype(BF16)

    await_bytes(slot_rows.at[pl.ds(0, HEADS - 1)], recv_sem.at[SLOTS])
    table_row = iota((table.shape[0], slots), 0).astype(F32)
    placed = jnp.concatenate(
        [
            jnp.where(table_row == slot_rows[i, 0:1, :], 1.0, 0.0).astype(BF16)
            for i in range(HEADS)
        ],
        axis=1,
    )

    def pass_beside(c):
        await_bytes(g_in.at[c, pl.ds(0, slots - chunk_rows), :], recv_sem.at[GX0 + c])
        spread(g_in.at[c], 0, slots, GY0 + 3 * c)

    for c in range(PARTS):
        pass_near(c, g_z, GZ0, g_x, g_in, seq * slots, GX0)
        if c > 0:
            pass_beside(c - 1)
        if c > 1:
            relay(g_in.at[c - 2], 0, slots, GY0 + 3 * (c - 2))
    pass_beside(PARTS - 1)
    for c in range(max(0, PARTS - 2), PARTS):
        relay(g_in.at[c], 0, slots, GY0 + 3 * c)
    for c in range(PARTS):
        settle(g_in.at[c], 0, slots, GY0 + 3 * c)
        grad_ref[:, c * part : (c + 1) * part] = mul_nn(placed, g_in[c])

    for group, view in leaving:
        await_bytes(view, send_sem.at[group])


def local(embedding_table, project_in, project_out, row_owner, row_offset, user_lengths, upstream):
    tokens = row_offset.shape[0]
    table_rows, width = embedding_table.shape
    ring = lax.axis_size("table") // PEERS
    group = tokens * HEADS
    slots = 2 * PEERS * ring
    part = width // PARTS
    head = width // HEADS
    vmem_spec = pl.BlockSpec(memory_space=pltpu.VMEM)
    hbm_spec = pl.BlockSpec(memory_space=pltpu.HBM)
    vmem = pltpu.VMEM
    return pl.pallas_call(
        functools.partial(kernel, ring),
        out_shape=(
            vmem((tokens, width), BF16),
            vmem((table_rows, width), F32),
        ),
        in_specs=[hbm_spec] * 7,
        out_specs=(vmem_spec, vmem_spec),
        scratch_shapes=[
            vmem((1, tokens), jnp.int32),
            vmem((1, tokens), jnp.int32),
            pltpu.SMEM((1, 3), jnp.int32),
            vmem((PEERS, 8, tokens), jnp.int32),
            vmem((ring, PEERS, tokens), jnp.int32),
            vmem((HEADS, 8, slots), F32),
            vmem((table_rows, width), BF16),
            vmem((width, 4 * width), BF16),
            vmem((width, width), BF16),
            vmem((group, width), BF16),
            vmem((4 * head, width), BF16),
            vmem((PARTS, slots, part), BF16),
            vmem((PARTS, slots, part), BF16),
            vmem((PARTS, slots, part), BF16),
            vmem((PARTS, slots, part), BF16),
            vmem((PARTS, group, part), BF16),
            vmem((group, width), BF16),
            vmem((4 * head, group), F32),
            vmem((4 * head, group), BF16),
            vmem((2, group, head), BF16),
            vmem((group, group), BF16),
            vmem((group, group), F32),
            vmem((head, group), F32),
            vmem((head, group), F32),
            vmem((HEADS, 8, group), F32),
            vmem((HEADS, head, tokens), BF16),
            vmem((width, tokens), BF16),
            vmem((HEADS, 4 * head, tokens), BF16),
            vmem((4 * width, tokens), BF16),
            vmem((width, tokens), F32),
            vmem((width, tokens), F32),
            vmem((PARTS, slots, part), BF16),
            vmem((PARTS, slots, part), BF16),
            vmem((PARTS, slots, part), BF16),
            vmem((PARTS, HEADS * slots, part), BF16),
            pltpu.SemaphoreType.DMA((7,)),
            pltpu.SemaphoreType.DMA((12 + 10 * PARTS,)),
            pltpu.SemaphoreType.DMA((12 + 10 * PARTS,)),
        ],
        compiler_params=pltpu.CompilerParams(
            collective_id=0, has_side_effects=True, vmem_limit_bytes=58 * 2**20
        ),
        name="hstu_step",
    )(
        row_owner.reshape(1, tokens),
        row_offset.reshape(1, tokens),
        user_lengths,
        embedding_table,
        project_in,
        project_out,
        upstream,
    )


def solution(mesh):
    return jax.shard_map(
        local,
        mesh=mesh,
        in_specs=(
            P("table", None),
            P(),
            P(),
            P(("table", "seq"), None),
            P(("table", "seq")),
            P("table", None),
            P(("table", "seq"), None),
        ),
        out_specs=(P(("table", "seq"), None), P("table", None)),
        check_vma=False,
    )
```

```python
import functools

import jax
import jax.numpy as jnp
from jax import lax
from jax.experimental import pallas as pl
from jax.experimental.pallas import tpu as pltpu
from jax.sharding import PartitionSpec as P

HEADS = 4
EPS = 1e-05
PEERS = 8
ROW_PARTS = 4
GRAD_PARTS = 4
F32 = jnp.float32
BF16 = jnp.bfloat16


def mul_nn(left, right):
    return lax.dot_general(left, right, (((1,), (0,)), ((), ())), preferred_element_type=F32)


def mul_nt(left, right):
    return lax.dot_general(left, right, (((1,), (1,)), ((), ())), preferred_element_type=F32)


def iota(shape, axis):
    return lax.broadcasted_iota(jnp.int32, shape, axis)


def kernel(
    ring,
    owner_hbm,
    offset_hbm,
    lengths_hbm,
    table_hbm,
    w_in_hbm,
    w_out_hbm,
    up_hbm,
    layer_ref,
    grad_ref,
    owner_v,
    offset_v,
    lengths,
    id_near,
    id_all,
    slot_rows,
    table,
    w_in,
    w_out,
    up_all,
    w_head,
    rows_out,
    rows_z,
    rows_x,
    rows_in,
    emb_all,
    normed_bf,
    pre,
    act,
    kv_rows,
    weights,
    slopes,
    grad_gated,
    attended,
    sums,
    gated_out,
    gated_in,
    gp_out,
    gp_in,
    normed_t,
    up_t,
    g_out,
    g_z,
    g_x,
    g_in,
    local_sem,
    send_sem,
    recv_sem,
):
    tokens = 128
    width = table.shape[1]
    head = width // HEADS
    row_part = width // ROW_PARTS
    grad_part = width // GRAD_PARTS
    slots = 2 * PEERS * ring
    block = 2 * PEERS
    chunk_rows = 2 * ring
    me = lax.axis_index("table")
    seq = lax.axis_index("seq")
    z = me // PEERS
    p = me % PEERS

    chip = p // 2
    core = p % 2

    def near_index(step):
        over, flip = ((1, 0), (3, 0), (1, 1), (3, 1), (2, 0), (2, 1), (0, 1), (0, 0))[step]
        return ((chip + over) % (PEERS // 2)) * 2 + (core + flip) % 2

    def near(step):
        return (z * PEERS + near_index(step), seq)

    around = [(near, beside) for beside in (2, 0, 1) for near in (4, 5, 0, 1, 2, 3, 6)]
    around = around[:2] + around[7:9] + around[14:16] + around[2:7] + around[9:14] + around[16:]
    around += [(near, 3) for near in range(PEERS - 1)]
    around += [(PEERS - 1, beside) for beside in (2, 0, 1)]

    def turn(i):
        hops = (ring - i) // 2
        odd = i % 2
        return z + odd * hops + (1 - odd) * (ring - hops)

    def far_index(i):
        return turn(i) % ring

    def far(i):
        return (far_index(i) * PEERS + p, seq)

    def beside_index(step):
        return (seq + (1, 3, 2, 0)[step]) % HEADS

    def beside(step):
        return (me, beside_index(step))

    leaving = []

    def send(src, dst, group, device):
        pltpu.make_async_remote_copy(
            src_ref=src,
            dst_ref=dst,
            send_sem=send_sem.at[group],
            recv_sem=recv_sem.at[group],
            device_id=device,
            device_id_type=pl.DeviceIdType.MESH,
        ).start()

    def await_bytes(view, sem):
        pltpu.make_async_copy(view, view, sem).wait()

    def rows(start, size):
        return pl.ds(pl.multiple_of(start, size), size)

    ID_NEAR, ID_FAR, SLOTS, SUMS, GATED = range(5)
    GP = 5
    UP = 9
    Z0 = 10
    X0 = Z0 + ROW_PARTS
    Y0 = X0 + ROW_PARTS
    GZ0 = Y0 + ROW_PARTS
    GX0 = GZ0 + GRAD_PARTS

    def spread_all(buf, start, size, group):
        mine = rows(start + seq * size, size)
        for step in range(HEADS - 1):
            send(buf.at[mine, :], buf.at[mine, :], group, beside(step))
        leaving.append((group, buf.at[pl.ds(start, 3 * size), :]))

    def settle_all(buf, start, size, group):
        await_bytes(buf.at[pl.ds(start, 3 * size), :], recv_sem.at[group])

    owner_copy = pltpu.make_async_copy(owner_hbm, owner_v, local_sem.at[4])
    owner_copy.start()
    offset_copy = pltpu.make_async_copy(offset_hbm, offset_v, local_sem.at[5])
    offset_copy.start()
    lengths_copy = pltpu.make_async_copy(lengths_hbm, lengths, local_sem.at[6])
    lengths_copy.start()
    up_copy = pltpu.make_async_copy(up_hbm, up_all.at[rows(seq * tokens, tokens), :], local_sem.at[0])
    up_copy.start()
    table_copy = pltpu.make_async_copy(table_hbm, table, local_sem.at[1])
    table_copy.start()
    in_copy = pltpu.make_async_copy(w_in_hbm, w_in, local_sem.at[2])
    in_copy.start()
    out_copy = pltpu.make_async_copy(w_out_hbm, w_out, local_sem.at[3])
    out_copy.start()

    barrier = pltpu.get_barrier_semaphore()
    for one, two in around:
        there = (z * PEERS + near_index(one), beside_index(two))
        pl.semaphore_signal(barrier, inc=1, device_id=there, device_id_type=pl.DeviceIdType.MESH)

    @pl.loop(0, ring - 1)
    def _(step):
        pl.semaphore_signal(barrier, inc=1, device_id=far(step), device_id_type=pl.DeviceIdType.MESH)

    owner_copy.wait()
    offset_copy.wait()
    owner = owner_v[...]
    code = owner * table.shape[0] + offset_v[...]
    id_near[p] = jnp.broadcast_to(code, (8, tokens))
    pl.semaphore_wait(barrier, len(around) + ring - 1)

    for step in range(PEERS - 1):
        send(id_near.at[p], id_near.at[p], ID_NEAR, near(step))
    leaving.append((ID_NEAR, id_near.at[pl.ds(0, PEERS - 1)]))

    owner_lane = jnp.broadcast_to(owner.astype(F32), (tokens, tokens))
    owner_sub = owner_lane.T
    n_sub = iota((tokens, tokens), 0)
    n_lane = iota((tokens, tokens), 1)
    same = owner_lane == owner_sub
    second_lane = jnp.max(jnp.where(same & (n_sub < n_lane), 1.0, 0.0), axis=0, keepdims=True)
    second_sub = jnp.max(jnp.where(same & (n_lane < n_sub), 1.0, 0.0), axis=1, keepdims=True)
    own_lane = owner
    slot_lane = (own_lane // PEERS) * block + second_lane.astype(jnp.int32) * PEERS + own_lane % PEERS
    own_sub = owner_sub[:, :1].astype(jnp.int32)
    slot_sub = (own_sub % PEERS) * chunk_rows + (own_sub // PEERS) * 2 + second_sub.astype(jnp.int32)
    pick_in = jnp.where(iota((tokens, slots), 1) == slot_sub, 1.0, 0.0).astype(BF16)
    place_out = jnp.where(iota((slots, tokens), 0) == slot_lane, 1.0, 0.0).astype(BF16)
    row_to = iota((slots, slots), 0)
    row_from = iota((slots, slots), 1)
    rest = row_to % chunk_rows
    source_row = (rest // 2) * block + (rest % 2) * PEERS + row_to // chunk_rows
    regroup = jnp.where(row_from == source_row, 1.0, 0.0).astype(BF16)

    await_bytes(id_near.at[pl.ds(0, PEERS - 1)], recv_sem.at[ID_NEAR])
    id_all[z] = jnp.concatenate([id_near[i, 0:1, :] for i in range(PEERS)], axis=0)

    @pl.loop(0, ring - 1)
    def _(step):
        send(id_all.at[z], id_all.at[z], ID_FAR, far(step))

    leaving.append((ID_FAR, id_all.at[pl.ds(0, ring - 1)]))
    up_copy.wait()
    spread_all(up_all, 0, tokens, UP)

    in_copy.wait()
    for i in range(4):
        columns = pl.ds(pl.multiple_of(i * width + seq * head, head), head)
        w_head[i * head : (i + 1) * head, :] = w_in[:, columns].T
    table_copy.wait()
    out_copy.wait()

    await_bytes(id_all.at[pl.ds(0, ring - 1)], recv_sem.at[ID_FAR])
    codes = id_all[...].reshape(ring * PEERS, tokens)
    wanted = (codes // table.shape[0]) == me
    offsets = (codes % table.shape[0]).astype(F32)
    place = iota((ring * PEERS, tokens), 1).astype(F32)
    first = jnp.min(jnp.where(wanted, place, 1000.0), axis=1, keepdims=True)
    last = jnp.max(jnp.where(wanted, place, -1.0), axis=1, keepdims=True)
    first_off = jnp.sum(jnp.where(place == first, offsets, 0.0), axis=1, keepdims=True)
    last_off = jnp.sum(jnp.where(place == last, offsets, 0.0), axis=1, keepdims=True)
    none = float(table.shape[0])
    first_off = jnp.where(first < 1000.0, first_off, none)
    last_off = jnp.where(last > first, last_off, none)
    row_id = iota((ring * PEERS, table.shape[0]), 1).astype(F32)

    def interleave(one, two):
        both = [x.reshape(ring, PEERS, x.shape[1]) for x in (one, two)]
        return jnp.concatenate(both, axis=1).reshape(slots, one.shape[1])

    chosen = interleave(
        jnp.where(row_id == first_off, 1.0, 0.0), jnp.where(row_id == last_off, 1.0, 0.0)
    ).astype(BF16)
    for c in range(ROW_PARTS):
        rows_out[c] = mul_nn(chosen, table[:, c * row_part : (c + 1) * row_part]).astype(BF16)
        mine = rows(z * block, block)

        @pl.loop(0, ring - 1)
        def _(step, c=c, mine=mine):
            there = rows(far_index(step) * block, block)
            send(rows_out.at[c, there, :], rows_z.at[c, mine, :], Z0 + c, far(step))

        leaving.append((Z0 + c, rows_z.at[c, pl.ds(0, slots - block), :]))

        rows_z[c, mine, :] = rows_out[c, mine, :]

    slot_off = interleave(
        jnp.broadcast_to(first_off, (ring * PEERS, tokens)),
        jnp.broadcast_to(last_off, (ring * PEERS, tokens)),
    ).T[:8]
    high = jnp.floor(slot_off * 0.0625)
    digits = jnp.concatenate([high, slot_off - 16.0 * high], axis=0).astype(BF16)
    moved = mul_nt(digits, regroup)
    slot_rows[seq] = moved[:8] * 16.0 + moved[8:]
    for step in range(HEADS - 1):
        send(slot_rows.at[seq], slot_rows.at[seq], SLOTS, beside(step))
    leaving.append((SLOTS, slot_rows.at[pl.ds(0, HEADS - 1)]))

    settle_all(up_all, 0, tokens, UP)
    grad_gated[...] = mul_nt(w_out[rows(seq * head, head), :], up_all[...])
    up_t[...] = up_all[rows(seq * tokens, tokens), :].astype(F32).T

    def pass_near(c, src, src_sem, mid, dst, base, sem):
        await_bytes(src.at[c, pl.ds(0, slots - block), :], recv_sem.at[src_sem + c])
        mid[c] = mul_nn(regroup, src[c]).astype(BF16)
        mine = rows(base + p * chunk_rows, chunk_rows)
        for step in range(PEERS - 1):
            there = rows(near_index(step) * chunk_rows, chunk_rows)
            send(mid.at[c, there, :], dst.at[c, mine, :], sem + c, near(step))
        leaving.append((sem + c, dst.at[c, pl.ds(0, slots - chunk_rows), :]))
        dst[c, mine, :] = mid[c, rows(p * chunk_rows, chunk_rows), :]

    def gather_rows(c):
        await_bytes(rows_in.at[c, pl.ds(0, slots - chunk_rows), :], recv_sem.at[X0 + c])
        mine = rows(seq * tokens, tokens)
        emb_all[c, mine, :] = mul_nn(pick_in, rows_in[c]).astype(BF16)
        spread_all(emb_all.at[c], 0, tokens, Y0 + c)

    for c in range(ROW_PARTS):
        pass_near(c, rows_z, Z0, rows_x, rows_in, 0, X0)
        if c > 0:
            gather_rows(c - 1)
    gather_rows(ROW_PARTS - 1)

    own = rows(seq * tokens, tokens)
    emb_own = jnp.concatenate([emb_all[c, own, :] for c in range(ROW_PARTS)], axis=1).astype(F32)
    emb_t = emb_own.T
    centered_t = emb_t - jnp.mean(emb_t, axis=0, keepdims=True)
    inv_own = lax.rsqrt(jnp.mean(centered_t * centered_t, axis=0, keepdims=True) + EPS)
    normed_t[...] = centered_t * inv_own

    for c in range(ROW_PARTS):
        settle_all(emb_all.at[c], 0, tokens, Y0 + c)
    for i in range(HEADS):
        here = slice(i * tokens, (i + 1) * tokens)
        wide = jnp.concatenate([emb_all[c, here, :] for c in range(ROW_PARTS)], axis=1).astype(F32)
        centered = wide - jnp.mean(wide, axis=1, keepdims=True)
        inv = lax.rsqrt(jnp.mean(centered * centered, axis=1, keepdims=True) + EPS)
        normed_bf[here, :] = (centered * inv).astype(BF16)

    pre[...] = mul_nt(w_head[...], normed_bf[...])
    for i in range(4):
        here = slice(i * head, (i + 1) * head)
        x = pre[here, :]
        act[here, :] = (x * jax.nn.sigmoid(x)).astype(BF16)
    gate = slice(0, head)
    value = slice(head, 2 * head)
    query = slice(2 * head, 3 * head)
    key = slice(3 * head, 4 * head)
    kv_rows[0] = act[value, :].T
    kv_rows[1] = act[key, :].T

    lengths_copy.wait()
    start_two = lengths[0, 0]
    start_three = start_two + lengths[0, 1]

    def user_of(position):
        return (position >= start_two).astype(jnp.int32) + (position >= start_three).astype(jnp.int32)

    scale = head ** (-0.5)
    blocks = [slice(i * tokens, (i + 1) * tokens) for i in range(HEADS)]

    def keys_of(j):
        return slice(max(0, j - 2) * tokens, (j + 1) * tokens)

    def queries_of(i):
        return slice(i * tokens, min(HEADS, i + 3) * tokens)

    for j in range(HEADS):
        here, ms = blocks[j], keys_of(j)
        count = ms.stop - ms.start
        scores = mul_nn(kv_rows[1, ms, :], act[query, here]) * scale
        m_at = iota((count, 1), 0) + ms.start
        n_at = iota((1, tokens), 1) + here.start
        allowed = (user_of(m_at) == user_of(n_at)) & (m_at <= n_at)
        logistic = jax.nn.sigmoid(scores)
        weight = jnp.where(allowed, scores * logistic, 0.0).astype(BF16)
        weights[ms, here] = weight
        slopes[ms, here] = jnp.where(
            allowed, logistic * (1.0 + scores * (1.0 - logistic)) * scale, 0.0
        )
        out = mul_nn(act[value, ms], weight)
        attended[:, here] = out
        g = grad_gated[:, here] * act[gate, here].astype(F32)
        out_mean = jnp.mean(out, axis=0, keepdims=True)
        g_mean = jnp.mean(g, axis=0, keepdims=True)
        out_c = out - out_mean
        out_sq = jnp.sum(out_c * out_c, axis=0, keepdims=True)
        cross = jnp.sum(out_c * (g - g_mean), axis=0, keepdims=True)
        sums[seq, :, here] = jnp.concatenate(
            [out_mean, out_sq, g_mean, cross, jnp.zeros((4, tokens), F32)], axis=0
        )
    for step in range(HEADS - 1):
        send(sums.at[seq], sums.at[seq], SUMS, beside(step))
    leaving.append((SUMS, sums.at[pl.ds(0, HEADS - 1)]))
    for i in range(4):
        here = slice(i * head, (i + 1) * head)
        x = pre[here, :]
        logistic = jax.nn.sigmoid(x)
        pre[here, :] = logistic * (1.0 + x * (1.0 - logistic))

    await_bytes(sums.at[pl.ds(0, HEADS - 1)], recv_sem.at[SUMS])
    parts = [sums[i] for i in range(HEADS)]
    means = [s[0:1] for s in parts]
    g_means = [s[2:3] for s in parts]
    out_mean = sum(means) * (1.0 / HEADS)
    g_mean = sum(g_means) * (1.0 / HEADS)
    out_sq = sum(s[1:2] for s in parts) + head * sum((m - out_mean) * (m - out_mean) for m in means)
    cross = sum(s[3:4] for s in parts) + head * sum(
        (m - out_mean) * (g - g_mean) for m, g in zip(means, g_means)
    )
    inv_out = lax.rsqrt(out_sq * (1.0 / width) + EPS)
    slant = inv_out * cross * (1.0 / width)

    def pre_slope(part_of, here):
        return pre[part_of, here]

    def exchange(i):
        here = pl.ds(i * head, head)
        mine = pl.ds(pl.multiple_of(i * width + seq * head, head), head)
        for step in range(HEADS - 1):
            there = beside_index(step)
            send(gp_out.at[there, here, :], gp_in.at[mine, :], GP + i, beside(step))
        leaving.append((GP + i, gp_in.at[pl.ds(i * width, 3 * head), :]))
        gp_in[mine, :] = gp_out[seq, here, :]

    grad_out = []
    for j in range(HEADS):
        here = blocks[j]
        gate_u = act[gate, here].astype(F32)
        raw = grad_gated[:, here]
        normed = (attended[:, here] - out_mean[:, here]) * inv_out[:, here]
        gated_out[j] = (normed * gate_u).astype(BF16)
        gp_out[j, gate, :] = (raw * normed * pre_slope(gate, here)).astype(BF16)
        grad_out.append(
            (
                inv_out[:, here]
                * (raw * gate_u - g_mean[:, here] - normed * slant[:, here])
            ).astype(BF16)
        )
    exchange(0)
    grad_out = jnp.concatenate(grad_out, axis=1)
    for i in range(HEADS):
        ns = queries_of(i)
        found = mul_nt(grad_out[:, ns], weights[blocks[i], ns])
        gp_out[i, value, :] = (found * pre_slope(value, blocks[i])).astype(BF16)
    exchange(1)
    grad_score = {}
    for j in range(HEADS):
        ms = keys_of(j)
        moved = mul_nn(kv_rows[0, ms, :], grad_out[:, blocks[j]])
        moved = (moved * slopes[ms, blocks[j]]).astype(BF16)
        grad_score[j] = moved
        weights[ms, blocks[j]] = moved
        found = mul_nn(act[key, ms], moved)
        gp_out[j, query, :] = (found * pre_slope(query, blocks[j])).astype(BF16)
    exchange(2)
    for i in range(HEADS):
        ns = queries_of(i)
        found = mul_nt(act[query, ns], weights[blocks[i], ns])
        gp_out[i, key, :] = (found * pre_slope(key, blocks[i])).astype(BF16)
    exchange(3)
    mine = rows(seq * head, head)
    for step in range(HEADS - 1):
        send(gated_out.at[beside_index(step)], gated_in.at[mine, :], GATED, beside(step))
    leaving.append((GATED, gated_in.at[pl.ds(0, 3 * head), :]))
    gated_in[mine, :] = gated_out[seq]

    grad_normed = jnp.zeros((width, tokens), F32)
    for i in range(4):
        await_bytes(gp_in.at[pl.ds(i * width, 3 * head), :], recv_sem.at[GP + i])
        here = slice(i * width, (i + 1) * width)
        grad_normed = grad_normed + mul_nn(w_in[:, here], gp_in[here, :])
    normed = normed_t[...]
    grad_rows = up_t[...] + inv_own * (
        grad_normed
        - jnp.mean(grad_normed, axis=0, keepdims=True)
        - normed * jnp.mean(grad_normed * normed, axis=0, keepdims=True)
    )
    grad_rows = grad_rows.astype(BF16)
    for c in range(GRAD_PARTS):
        g_out[c] = mul_nt(place_out, grad_rows[c * grad_part : (c + 1) * grad_part]).astype(BF16)
        mine = rows(z * block, block)

        @pl.loop(0, ring - 1)
        def _(step, c=c, mine=mine):
            there = rows(far_index(step) * block, block)
            send(g_out.at[c, there, :], g_z.at[c, mine, :], GZ0 + c, far(step))

        leaving.append((GZ0 + c, g_z.at[c, pl.ds(0, slots - block), :]))

        g_z[c, mine, :] = g_out[c, mine, :]

    await_bytes(gated_in.at[pl.ds(0, 3 * head), :], recv_sem.at[GATED])
    layer_ref[...] = (emb_own + mul_nn(gated_in[...].T, w_out[...])).astype(BF16)

    await_bytes(slot_rows.at[pl.ds(0, HEADS - 1)], recv_sem.at[SLOTS])
    table_row = iota((table.shape[0], slots), 0).astype(F32)
    placed = jnp.concatenate(
        [
            jnp.where(table_row == slot_rows[i, 0:1, :], 1.0, 0.0).astype(BF16)
            for i in range(HEADS)
        ],
        axis=1,
    )

    mine = rows(seq * slots + p * chunk_rows, chunk_rows)
    for c in range(GRAD_PARTS):
        await_bytes(g_z.at[c, pl.ds(0, slots - block), :], recv_sem.at[GZ0 + c])
        g_x[c] = mul_nn(regroup, g_z[c]).astype(BF16)
        for one, two in around:
            to = near_index(one)
            there = rows(to * chunk_rows, chunk_rows)
            device = (z * PEERS + to, beside_index(two))
            send(g_x.at[c, there, :], g_in.at[c, mine, :], GX0 + c, device)
        leaving.append((GX0 + c, g_in.at[c, pl.ds(0, HEADS * slots - chunk_rows), :]))
        g_in[c, mine, :] = g_x[c, rows(p * chunk_rows, chunk_rows), :]
    for c in range(GRAD_PARTS):
        await_bytes(g_in.at[c, pl.ds(0, HEADS * slots - chunk_rows), :], recv_sem.at[GX0 + c])
        grad_ref[:, c * grad_part : (c + 1) * grad_part] = mul_nn(placed, g_in[c])

    for group, view in leaving:
        await_bytes(view, send_sem.at[group])


def local(embedding_table, project_in, project_out, row_owner, row_offset, user_lengths, upstream):
    tokens = row_offset.shape[0]
    table_rows, width = embedding_table.shape
    ring = lax.axis_size("table") // PEERS
    group = tokens * HEADS
    slots = 2 * PEERS * ring
    head = width // HEADS
    vmem_spec = pl.BlockSpec(memory_space=pltpu.VMEM)
    hbm_spec = pl.BlockSpec(memory_space=pltpu.HBM)
    vmem = pltpu.VMEM
    return pl.pallas_call(
        functools.partial(kernel, ring),
        out_shape=(
            vmem((tokens, width), BF16),
            vmem((table_rows, width), F32),
        ),
        in_specs=[hbm_spec] * 7,
        out_specs=(vmem_spec, vmem_spec),
        scratch_shapes=[
            vmem((1, tokens), jnp.int32),
            vmem((1, tokens), jnp.int32),
            pltpu.SMEM((1, 3), jnp.int32),
            vmem((PEERS, 8, tokens), jnp.int32),
            vmem((ring, PEERS, tokens), jnp.int32),
            vmem((HEADS, 8, slots), F32),
            vmem((table_rows, width), BF16),
            vmem((width, 4 * width), BF16),
            vmem((width, width), BF16),
            vmem((group, width), BF16),
            vmem((4 * head, width), BF16),
            vmem((ROW_PARTS, slots, width // ROW_PARTS), BF16),
            vmem((ROW_PARTS, slots, width // ROW_PARTS), BF16),
            vmem((ROW_PARTS, slots, width // ROW_PARTS), BF16),
            vmem((ROW_PARTS, slots, width // ROW_PARTS), BF16),
            vmem((ROW_PARTS, group, width // ROW_PARTS), BF16),
            vmem((group, width), BF16),
            vmem((4 * head, group), F32),
            vmem((4 * head, group), BF16),
            vmem((2, group, head), BF16),
            vmem((group, group), BF16),
            vmem((group, group), F32),
            vmem((head, group), F32),
            vmem((head, group), F32),
            vmem((HEADS, 8, group), F32),
            vmem((HEADS, head, tokens), BF16),
            vmem((width, tokens), BF16),
            vmem((HEADS, 4 * head, tokens), BF16),
            vmem((4 * width, tokens), BF16),
            vmem((width, tokens), F32),
            vmem((width, tokens), F32),
            vmem((GRAD_PARTS, slots, width // GRAD_PARTS), BF16),
            vmem((GRAD_PARTS, slots, width // GRAD_PARTS), BF16),
            vmem((GRAD_PARTS, slots, width // GRAD_PARTS), BF16),
            vmem((GRAD_PARTS, HEADS * slots, width // GRAD_PARTS), BF16),
            pltpu.SemaphoreType.DMA((7,)),
            pltpu.SemaphoreType.DMA((10 + 3 * ROW_PARTS + 2 * GRAD_PARTS,)),
            pltpu.SemaphoreType.DMA((10 + 3 * ROW_PARTS + 2 * GRAD_PARTS,)),
        ],
        compiler_params=pltpu.CompilerParams(
            collective_id=0, has_side_effects=True, vmem_limit_bytes=58 * 2**20
        ),
        name="hstu_step",
    )(
        row_owner.reshape(1, tokens),
        row_offset.reshape(1, tokens),
        user_lengths,
        embedding_table,
        project_in,
        project_out,
        upstream,
    )


def solution(mesh):
    return jax.shard_map(
        local,
        mesh=mesh,
        in_specs=(
            P("table", None),
            P(),
            P(),
            P(("table", "seq"), None),
            P(("table", "seq")),
            P("table", None),
            P(("table", "seq"), None),
        ),
        out_specs=(P(("table", "seq"), None), P("table", None)),
        check_vma=False,
    )
```

```python
import functools

import jax
import jax.numpy as jnp
from jax import lax
from jax.experimental import pallas as pl
from jax.experimental.pallas import tpu as pltpu
from jax.sharding import PartitionSpec as P

HEADS = 4
EPS = 1e-05
PEERS = 8
ROW_PARTS = 4
GRAD_PARTS = 4
F32 = jnp.float32
BF16 = jnp.bfloat16


def mul_nn(left, right):
    return lax.dot_general(left, right, (((1,), (0,)), ((), ())), preferred_element_type=F32)


def mul_nt(left, right):
    return lax.dot_general(left, right, (((1,), (1,)), ((), ())), preferred_element_type=F32)


def iota(shape, axis):
    return lax.broadcasted_iota(jnp.int32, shape, axis)


def kernel(
    ring,
    owner_hbm,
    offset_hbm,
    lengths_hbm,
    table_hbm,
    w_in_hbm,
    w_out_hbm,
    up_hbm,
    layer_ref,
    grad_ref,
    owner_v,
    offset_v,
    lengths,
    id_near,
    id_seq,
    id_all,
    slot_rows,
    table,
    w_in,
    w_out,
    up_all,
    w_head,
    rows_out,
    rows_z,
    rows_x,
    rows_in,
    emb_all,
    normed_bf,
    pre,
    act,
    kv_rows,
    weights,
    slopes,
    grad_gated,
    attended,
    grad_out,
    gated,
    gp_in,
    normed_t,
    up_t,
    g_out,
    g_z,
    g_x,
    g_in,
    local_sem,
    send_sem,
    recv_sem,
):
    tokens = 128
    width = table.shape[1]
    head = width // HEADS
    row_part = width // ROW_PARTS
    grad_part = width // GRAD_PARTS
    slots = 2 * PEERS * ring
    block = 2 * PEERS
    chunk_rows = 2 * ring
    me = lax.axis_index("table")
    seq = lax.axis_index("seq")
    z = me // PEERS
    p = me % PEERS

    chip = p // 2
    core = p % 2

    def near_index(step):
        over, flip = ((1, 0), (3, 0), (1, 1), (3, 1), (2, 0), (2, 1), (0, 1), (0, 0))[step]
        return ((chip + over) % (PEERS // 2)) * 2 + (core + flip) % 2

    def near(step):
        return (z * PEERS + near_index(step), seq)

    around = [(near, beside) for beside in (2, 0, 1) for near in (4, 5, 0, 1, 2, 3, 6)]
    around = around[:2] + around[7:9] + around[14:16] + around[2:7] + around[9:14] + around[16:]
    around += [(near, 3) for near in range(PEERS - 1)]
    around += [(PEERS - 1, beside) for beside in (2, 0, 1)]

    def turn(i):
        hops = (ring - i) // 2
        odd = i % 2
        return z + odd * hops + (1 - odd) * (ring - hops)

    def far_index(i):
        return turn(i) % ring

    def far(i):
        return (far_index(i) * PEERS + p, seq)

    def beside_index(step):
        return (seq + (1, 3, 2, 0)[step]) % HEADS

    def beside(step):
        return (me, beside_index(step))

    leaving = []

    def send(src, dst, group, device):
        pltpu.make_async_remote_copy(
            src_ref=src,
            dst_ref=dst,
            send_sem=send_sem.at[group],
            recv_sem=recv_sem.at[group],
            device_id=device,
            device_id_type=pl.DeviceIdType.MESH,
        ).start()

    def await_bytes(view, sem):
        pltpu.make_async_copy(view, view, sem).wait()

    def rows(start, size):
        return pl.ds(pl.multiple_of(start, size), size)

    ID_NEAR, ID_FAR, ID_SEQ, SLOTS, UP = range(5)
    Z0 = 5
    X0 = Z0 + ROW_PARTS
    GZ0 = X0 + ROW_PARTS
    GX0 = GZ0 + GRAD_PARTS

    def spread_all(buf, start, size, group):
        mine = rows(start + seq * size, size)
        for step in range(HEADS - 1):
            send(buf.at[mine, :], buf.at[mine, :], group, beside(step))
        leaving.append((group, buf.at[pl.ds(start, 3 * size), :]))

    def settle_all(buf, start, size, group):
        await_bytes(buf.at[pl.ds(start, 3 * size), :], recv_sem.at[group])

    owner_copy = pltpu.make_async_copy(owner_hbm, owner_v, local_sem.at[4])
    owner_copy.start()
    offset_copy = pltpu.make_async_copy(offset_hbm, offset_v, local_sem.at[5])
    offset_copy.start()
    lengths_copy = pltpu.make_async_copy(lengths_hbm, lengths, local_sem.at[6])
    lengths_copy.start()
    up_copy = pltpu.make_async_copy(up_hbm, up_all.at[rows(seq * tokens, tokens), :], local_sem.at[0])
    up_copy.start()
    table_copy = pltpu.make_async_copy(table_hbm, table, local_sem.at[1])
    table_copy.start()
    in_copy = pltpu.make_async_copy(w_in_hbm, w_in, local_sem.at[2])
    in_copy.start()
    out_copy = pltpu.make_async_copy(w_out_hbm, w_out, local_sem.at[3])
    out_copy.start()

    barrier = pltpu.get_barrier_semaphore()
    @pl.loop(0, ring - 1)
    def _(step):
        pl.semaphore_signal(barrier, inc=1, device_id=far(step), device_id_type=pl.DeviceIdType.MESH)

    for one, two in around:
        there = (z * PEERS + near_index(one), beside_index(two))
        pl.semaphore_signal(barrier, inc=1, device_id=there, device_id_type=pl.DeviceIdType.MESH)

    owner_copy.wait()
    offset_copy.wait()
    owner = owner_v[...]
    code = owner * table.shape[0] + offset_v[...]
    id_near[p] = jnp.broadcast_to(code, (8, tokens))
    id_seq[seq] = id_near[p]
    pl.semaphore_wait(barrier, len(around) + ring - 1)

    for step in range(PEERS - 1):
        send(id_near.at[p], id_near.at[p], ID_NEAR, near(step))
    leaving.append((ID_NEAR, id_near.at[pl.ds(0, PEERS - 1)]))
    for step in range(HEADS - 1):
        send(id_seq.at[seq], id_seq.at[seq], ID_SEQ, beside(step))
    leaving.append((ID_SEQ, id_seq.at[pl.ds(0, HEADS - 1)]))

    n_sub = iota((tokens, tokens), 0)
    n_lane = iota((tokens, tokens), 1)

    def both_ways(owners):
        wide = jnp.broadcast_to(owners.astype(F32), (tokens, tokens))
        return wide, wide.T

    owner_lane, owner_sub = both_ways(owner)
    second_lane = jnp.max(
        jnp.where((owner_lane == owner_sub) & (n_sub < n_lane), 1.0, 0.0), axis=0, keepdims=True
    )
    slot_lane = (owner // PEERS) * block + second_lane.astype(jnp.int32) * PEERS + owner % PEERS
    place_out = jnp.where(iota((slots, tokens), 0) == slot_lane, 1.0, 0.0).astype(BF16)

    def picker(owners):
        lane, sub = both_ways(owners)
        second = jnp.max(
            jnp.where((lane == sub) & (n_lane < n_sub), 1.0, 0.0), axis=1, keepdims=True
        ).astype(jnp.int32)
        owner_of = sub[:, :1].astype(jnp.int32)
        slot = (owner_of % PEERS) * chunk_rows + (owner_of // PEERS) * 2 + second
        return jnp.where(iota((tokens, slots), 1) == slot, 1.0, 0.0).astype(BF16)

    row_to = iota((slots, slots), 0)
    row_from = iota((slots, slots), 1)
    rest = row_to % chunk_rows
    source_row = (rest // 2) * block + (rest % 2) * PEERS + row_to // chunk_rows
    regroup = jnp.where(row_from == source_row, 1.0, 0.0).astype(BF16)

    await_bytes(id_near.at[pl.ds(0, PEERS - 1)], recv_sem.at[ID_NEAR])
    id_all[z] = jnp.concatenate([id_near[i, 0:1, :] for i in range(PEERS)], axis=0)

    @pl.loop(0, ring - 1)
    def _(step):
        send(id_all.at[z], id_all.at[z], ID_FAR, far(step))

    leaving.append((ID_FAR, id_all.at[pl.ds(0, ring - 1)]))
    up_copy.wait()
    spread_all(up_all, 0, tokens, UP)

    in_copy.wait()
    for i in range(4 * HEADS):
        columns = slice(i * head, (i + 1) * head)
        w_head[columns, :] = w_in[:, columns].T
    group = HEADS * tokens
    edge = 2 * tokens
    act[:, :edge] = jnp.zeros((4 * width, edge), BF16)
    act[:, edge + group :] = jnp.zeros((4 * width, edge), BF16)
    grad_out[:, group:] = jnp.zeros((width, edge), BF16)
    for h in range(HEADS):
        kv_rows[0, h, :edge, :] = jnp.zeros((edge, head), BF16)
        weights[h, edge:, group:] = jnp.zeros((group, edge), BF16)
        slopes[h, edge:, group:] = jnp.zeros((group, edge), F32)
        slopes[h, :edge, :group] = jnp.zeros((edge, group), F32)
    table_copy.wait()
    out_copy.wait()

    await_bytes(id_all.at[pl.ds(0, ring - 1)], recv_sem.at[ID_FAR])
    codes = id_all[...].reshape(ring * PEERS, tokens)
    wanted = (codes // table.shape[0]) == me
    offsets = (codes % table.shape[0]).astype(F32)
    place = iota((ring * PEERS, tokens), 1).astype(F32)
    first = jnp.min(jnp.where(wanted, place, 1000.0), axis=1, keepdims=True)
    last = jnp.max(jnp.where(wanted, place, -1.0), axis=1, keepdims=True)
    first_off = jnp.sum(jnp.where(place == first, offsets, 0.0), axis=1, keepdims=True)
    last_off = jnp.sum(jnp.where(place == last, offsets, 0.0), axis=1, keepdims=True)
    none = float(table.shape[0])
    first_off = jnp.where(first < 1000.0, first_off, none)
    last_off = jnp.where(last > first, last_off, none)
    row_id = iota((ring * PEERS, table.shape[0]), 1).astype(F32)

    def interleave(one, two):
        both = [x.reshape(ring, PEERS, x.shape[1]) for x in (one, two)]
        return jnp.concatenate(both, axis=1).reshape(slots, one.shape[1])

    chosen = interleave(
        jnp.where(row_id == first_off, 1.0, 0.0), jnp.where(row_id == last_off, 1.0, 0.0)
    ).astype(BF16)
    for c in range(ROW_PARTS):
        rows_out[c] = mul_nn(chosen, table[:, c * row_part : (c + 1) * row_part]).astype(BF16)
        mine = rows(z * block, block)

        @pl.loop(0, ring - 1)
        def _(step, c=c, mine=mine):
            there = rows(far_index(step) * block, block)
            send(rows_out.at[c, there, :], rows_z.at[c, mine, :], Z0 + c, far(step))

        leaving.append((Z0 + c, rows_z.at[c, pl.ds(0, slots - block), :]))

        rows_z[c, mine, :] = rows_out[c, mine, :]

    slot_off = interleave(
        jnp.broadcast_to(first_off, (ring * PEERS, tokens)),
        jnp.broadcast_to(last_off, (ring * PEERS, tokens)),
    ).T[:8]
    high = jnp.floor(slot_off * 0.0625)
    digits = jnp.concatenate([high, slot_off - 16.0 * high], axis=0).astype(BF16)
    moved = mul_nt(digits, regroup)
    slot_rows[seq] = moved[:8] * 16.0 + moved[8:]
    for step in range(HEADS - 1):
        send(slot_rows.at[seq], slot_rows.at[seq], SLOTS, beside(step))
    leaving.append((SLOTS, slot_rows.at[pl.ds(0, HEADS - 1)]))

    settle_all(up_all, 0, tokens, UP)
    grad_gated[...] = mul_nt(w_out[...], up_all[...])
    up_t[...] = up_all[rows(seq * tokens, tokens), :].astype(F32).T
    await_bytes(id_seq.at[pl.ds(0, HEADS - 1)], recv_sem.at[ID_SEQ])
    pick_in = [picker(id_seq[i, 0:1, :] // table.shape[0]) for i in range(HEADS)]

    def pass_around(c, src, src_sem, mid, dst, sem):
        await_bytes(src.at[c, pl.ds(0, slots - block), :], recv_sem.at[src_sem + c])
        mid[c] = mul_nn(regroup, src[c]).astype(BF16)
        mine = rows(seq * slots + p * chunk_rows, chunk_rows)
        for one, two in around:
            to = near_index(one)
            there = rows(to * chunk_rows, chunk_rows)
            device = (z * PEERS + to, beside_index(two))
            send(mid.at[c, there, :], dst.at[c, mine, :], sem + c, device)
        leaving.append((sem + c, dst.at[c, pl.ds(0, HEADS * slots - chunk_rows), :]))
        dst[c, mine, :] = mid[c, rows(p * chunk_rows, chunk_rows), :]

    def arrive_around(c, dst, sem):
        await_bytes(dst.at[c, pl.ds(0, HEADS * slots - chunk_rows), :], recv_sem.at[sem + c])

    for c in range(ROW_PARTS):
        pass_around(c, rows_z, Z0, rows_x, rows_in, X0)
    for c in range(ROW_PARTS):
        arrive_around(c, rows_in, X0)
        for i in range(HEADS):
            found = mul_nn(pick_in[i], rows_in[c, i * slots : (i + 1) * slots, :])
            emb_all[c, i * tokens : (i + 1) * tokens, :] = found.astype(BF16)

    own = rows(seq * tokens, tokens)
    emb_own = jnp.concatenate([emb_all[c, own, :] for c in range(ROW_PARTS)], axis=1).astype(F32)
    emb_t = emb_own.T
    centered_t = emb_t - jnp.mean(emb_t, axis=0, keepdims=True)
    inv_own = lax.rsqrt(jnp.mean(centered_t * centered_t, axis=0, keepdims=True) + EPS)
    normed_t[...] = centered_t * inv_own

    for i in range(HEADS):
        here = slice(i * tokens, (i + 1) * tokens)
        wide = jnp.concatenate([emb_all[c, here, :] for c in range(ROW_PARTS)], axis=1).astype(F32)
        centered = wide - jnp.mean(wide, axis=1, keepdims=True)
        inv = lax.rsqrt(jnp.mean(centered * centered, axis=1, keepdims=True) + EPS)
        normed_bf[here, :] = (centered * inv).astype(BF16)

    pre[...] = mul_nt(w_head[...], normed_bf[...])
    inside = slice(edge, edge + group)

    def head_of(i, h):
        return slice(i * width + h * head, i * width + (h + 1) * head)

    for i in range(4):
        for h in range(HEADS):
            x = pre[head_of(i, h), :]
            found = (x * jax.nn.sigmoid(x)).astype(BF16)
            act[head_of(i, h), inside] = found
            if i == 1:
                kv_rows[0, h, inside, :] = found.T
            if i == 3:
                kv_rows[1, h, inside, :] = found.T
    GATE, VALUE, QUERY, KEY = range(4)

    lengths_copy.wait()
    start_two = lengths[0, 0]
    start_three = start_two + lengths[0, 1]

    def user_of(position):
        return (position >= start_two).astype(jnp.int32) + (position >= start_three).astype(jnp.int32)

    scale = head ** (-0.5)
    for j in range(HEADS):
        low = max(0, j - 2) * tokens
        count = (j + 1) * tokens - low
        here = slice(j * tokens, (j + 1) * tokens)
        here_in = slice(edge + j * tokens, edge + (j + 1) * tokens)
        ms_in = slice(edge + low, edge + low + count)
        m_at = iota((count, 1), 0) + low
        n_at = iota((1, tokens), 1) + j * tokens
        allowed = (user_of(m_at) == user_of(n_at)) & (m_at <= n_at)
        for h in range(HEADS):
            scores = mul_nn(kv_rows[1, h, ms_in, :], act[head_of(QUERY, h), here_in]) * scale
            logistic = jax.nn.sigmoid(scores)
            weight = jnp.where(allowed, scores * logistic, 0.0).astype(BF16)
            weights[h, ms_in, here] = weight
            slopes[h, ms_in, here] = jnp.where(
                allowed, logistic * (1.0 + scores * (1.0 - logistic)) * scale, 0.0
            )
            attended[head_of(0, h), here] = mul_nn(act[head_of(VALUE, h), ms_in], weight)
        out = attended[:, here]
        g = grad_gated[:, here] * act[:width, here_in].astype(F32)
        out = out - jnp.mean(out, axis=0, keepdims=True)
        inv_out = lax.rsqrt(jnp.mean(out * out, axis=0, keepdims=True) + EPS)
        out = out * inv_out
        attended[:, here] = out
        slant = jnp.mean(g * out, axis=0, keepdims=True)
        grad_out[:, here] = (
            inv_out * (g - jnp.mean(g, axis=0, keepdims=True) - out * slant)
        ).astype(BF16)

    at = pl.multiple_of(seq * tokens, tokens)
    own_n = pl.ds(at, tokens)
    own_in = pl.ds(pl.multiple_of(edge + at, tokens), tokens)
    reach = pl.ds(at, 3 * tokens)
    later_in = pl.ds(pl.multiple_of(edge + at, tokens), 3 * tokens)

    def slope(part_of):
        x = pre[part_of, own_n]
        logistic = jax.nn.sigmoid(x)
        return logistic * (1.0 + x * (1.0 - logistic))

    normed_out = attended[:, own_n]
    gated[...] = (normed_out * act[:width, own_in].astype(F32)).astype(BF16)
    gate = slice(0, width)
    gp_in[gate, :] = (grad_gated[:, own_n] * normed_out * slope(gate)).astype(BF16)
    for h in range(HEADS):
        of_head = head_of(0, h)
        grad_later = grad_out[of_head, reach]
        found = mul_nt(grad_later, weights[h, own_in, reach])
        to = head_of(VALUE, h)
        gp_in[to, :] = (found * slope(to)).astype(BF16)
        score = mul_nn(kv_rows[0, h, reach, :], grad_out[of_head, own_n])
        score = (score * slopes[h, reach, own_n]).astype(BF16)
        found = mul_nn(act[head_of(KEY, h), reach], score)
        to = head_of(QUERY, h)
        gp_in[to, :] = (found * slope(to)).astype(BF16)
        score = mul_nn(kv_rows[0, h, own_in, :], grad_later)
        score = (score * slopes[h, own_in, reach]).astype(BF16)
        found = mul_nt(act[head_of(QUERY, h), later_in], score)
        to = head_of(KEY, h)
        gp_in[to, :] = (found * slope(to)).astype(BF16)

    grad_normed = mul_nn(w_in[...], gp_in[...])
    normed = normed_t[...]
    grad_rows = up_t[...] + inv_own * (
        grad_normed
        - jnp.mean(grad_normed, axis=0, keepdims=True)
        - normed * jnp.mean(grad_normed * normed, axis=0, keepdims=True)
    )
    grad_rows = grad_rows.astype(BF16)
    for c in range(GRAD_PARTS):
        g_out[c] = mul_nt(place_out, grad_rows[c * grad_part : (c + 1) * grad_part]).astype(BF16)
        mine = rows(z * block, block)

        @pl.loop(0, ring - 1)
        def _(step, c=c, mine=mine):
            there = rows(far_index(step) * block, block)
            send(g_out.at[c, there, :], g_z.at[c, mine, :], GZ0 + c, far(step))

        leaving.append((GZ0 + c, g_z.at[c, pl.ds(0, slots - block), :]))

        g_z[c, mine, :] = g_out[c, mine, :]

    layer_ref[...] = (emb_own + mul_nn(gated[...].T, w_out[...])).astype(BF16)

    await_bytes(slot_rows.at[pl.ds(0, HEADS - 1)], recv_sem.at[SLOTS])
    table_row = iota((table.shape[0], slots), 0).astype(F32)
    placed = jnp.concatenate(
        [
            jnp.where(table_row == slot_rows[i, 0:1, :], 1.0, 0.0).astype(BF16)
            for i in range(HEADS)
        ],
        axis=1,
    )

    for c in range(GRAD_PARTS):
        pass_around(c, g_z, GZ0, g_x, g_in, GX0)
    for c in range(GRAD_PARTS):
        arrive_around(c, g_in, GX0)
        grad_ref[:, c * grad_part : (c + 1) * grad_part] = mul_nn(placed, g_in[c])

    for group, view in leaving:
        await_bytes(view, send_sem.at[group])


def local(embedding_table, project_in, project_out, row_owner, row_offset, user_lengths, upstream):
    tokens = row_offset.shape[0]
    table_rows, width = embedding_table.shape
    ring = lax.axis_size("table") // PEERS
    group = tokens * HEADS
    slots = 2 * PEERS * ring
    head = width // HEADS
    vmem_spec = pl.BlockSpec(memory_space=pltpu.VMEM)
    hbm_spec = pl.BlockSpec(memory_space=pltpu.HBM)
    vmem = pltpu.VMEM
    return pl.pallas_call(
        functools.partial(kernel, ring),
        out_shape=(
            vmem((tokens, width), BF16),
            vmem((table_rows, width), F32),
        ),
        in_specs=[hbm_spec] * 7,
        out_specs=(vmem_spec, vmem_spec),
        scratch_shapes=[
            vmem((1, tokens), jnp.int32),
            vmem((1, tokens), jnp.int32),
            pltpu.SMEM((1, 3), jnp.int32),
            vmem((PEERS, 8, tokens), jnp.int32),
            vmem((HEADS, 8, tokens), jnp.int32),
            vmem((ring, PEERS, tokens), jnp.int32),
            vmem((HEADS, 8, slots), F32),
            vmem((table_rows, width), BF16),
            vmem((width, 4 * width), BF16),
            vmem((width, width), BF16),
            vmem((group, width), BF16),
            vmem((4 * width, width), BF16),
            vmem((ROW_PARTS, slots, width // ROW_PARTS), BF16),
            vmem((ROW_PARTS, slots, width // ROW_PARTS), BF16),
            vmem((ROW_PARTS, slots, width // ROW_PARTS), BF16),
            vmem((ROW_PARTS, HEADS * slots, width // ROW_PARTS), BF16),
            vmem((ROW_PARTS, group, width // ROW_PARTS), BF16),
            vmem((group, width), BF16),
            vmem((4 * width, group), F32),
            vmem((4 * width, 2 * group), BF16),
            vmem((2, HEADS, group + 2 * tokens, head), BF16),
            vmem((HEADS, group + 2 * tokens, group + 2 * tokens), BF16),
            vmem((HEADS, group + 2 * tokens, group + 2 * tokens), F32),
            vmem((width, group), F32),
            vmem((width, group), F32),
            vmem((width, group + 2 * tokens), BF16),
            vmem((width, tokens), BF16),
            vmem((4 * width, tokens), BF16),
            vmem((width, tokens), F32),
            vmem((width, tokens), F32),
            vmem((GRAD_PARTS, slots, width // GRAD_PARTS), BF16),
            vmem((GRAD_PARTS, slots, width // GRAD_PARTS), BF16),
            vmem((GRAD_PARTS, slots, width // GRAD_PARTS), BF16),
            vmem((GRAD_PARTS, HEADS * slots, width // GRAD_PARTS), BF16),
            pltpu.SemaphoreType.DMA((7,)),
            pltpu.SemaphoreType.DMA((5 + 2 * ROW_PARTS + 2 * GRAD_PARTS,)),
            pltpu.SemaphoreType.DMA((5 + 2 * ROW_PARTS + 2 * GRAD_PARTS,)),
        ],
        compiler_params=pltpu.CompilerParams(
            collective_id=0, has_side_effects=True, vmem_limit_bytes=58 * 2**20
        ),
        name="hstu_step",
    )(
        row_owner.reshape(1, tokens),
        row_offset.reshape(1, tokens),
        user_lengths,
        embedding_table,
        project_in,
        project_out,
        upstream,
    )


def solution(mesh):
    return jax.shard_map(
        local,
        mesh=mesh,
        in_specs=(
            P("table", None),
            P(),
            P(),
            P(("table", "seq"), None),
            P(("table", "seq")),
            P("table", None),
            P(("table", "seq"), None),
        ),
        out_specs=(P(("table", "seq"), None), P("table", None)),
        check_vma=False,
    )
```

```python
import functools

import jax
import jax.numpy as jnp
from jax import lax
from jax.experimental import pallas as pl
from jax.experimental.pallas import tpu as pltpu
from jax.sharding import PartitionSpec as P

HEADS = 4
EPS = 1e-05
PEERS = 8
ROW_PARTS = 4
GRAD_PARTS = 4
F32 = jnp.float32
BF16 = jnp.bfloat16


def mul_nn(left, right):
    return lax.dot_general(left, right, (((1,), (0,)), ((), ())), preferred_element_type=F32)


def mul_nt(left, right):
    return lax.dot_general(left, right, (((1,), (1,)), ((), ())), preferred_element_type=F32)


def iota(shape, axis):
    return lax.broadcasted_iota(jnp.int32, shape, axis)


def kernel(
    ring,
    owner_hbm,
    offset_hbm,
    lengths_hbm,
    table_hbm,
    w_in_hbm,
    w_out_hbm,
    up_hbm,
    layer_ref,
    grad_ref,
    owner_v,
    offset_v,
    lengths,
    id_near,
    id_seq,
    id_all,
    slot_rows,
    table,
    w_in,
    w_out,
    up_all,
    w_head,
    rows_out,
    rows_z,
    rows_x,
    rows_in,
    emb_all,
    normed_bf,
    pre,
    act,
    kv_rows,
    weights,
    slopes,
    grad_gated,
    attended,
    grad_out,
    gp_in,
    normed_t,
    up_t,
    g_out,
    g_z,
    g_x,
    g_in,
    local_sem,
    send_sem,
    recv_sem,
):
    tokens = 128
    width = table.shape[1]
    head = width // HEADS
    row_part = width // ROW_PARTS
    grad_part = width // GRAD_PARTS
    slots = 2 * PEERS * ring
    block = 2 * PEERS
    chunk_rows = 2 * ring
    me = lax.axis_index("table")
    seq = lax.axis_index("seq")
    z = me // PEERS
    p = me % PEERS

    chip = p // 2
    core = p % 2

    def near_index(step):
        over, flip = ((1, 0), (3, 0), (1, 1), (3, 1), (2, 0), (2, 1), (0, 1), (0, 0))[step]
        return ((chip + over) % (PEERS // 2)) * 2 + (core + flip) % 2

    def near(step):
        return (z * PEERS + near_index(step), seq)

    every = [(i % PEERS, i // PEERS) for i in range(PEERS * HEADS - 1)]
    mixed = [every[13 * i % len(every)] for i in range(len(every))]
    hops = [(1, 1, 1, 1, 2, 2, 0, 0)[one] + (1, 1, 2, 0)[two] for one, two in mixed]
    around = [pair for far in (4, 3, 2, 1, 0) for pair, h in zip(mixed, hops) if h == far]

    def turn(i):
        hops = (ring - i) // 2
        odd = i % 2
        return z + odd * hops + (1 - odd) * (ring - hops)

    def far_index(i):
        return turn(i) % ring

    def far(i):
        return (far_index(i) * PEERS + p, seq)

    def beside_index(step):
        return (seq + (1, 3, 2, 0)[step]) % HEADS

    def beside(step):
        return (me, beside_index(step))

    leaving = []

    def send(src, dst, group, device):
        pltpu.make_async_remote_copy(
            src_ref=src,
            dst_ref=dst,
            send_sem=send_sem.at[group],
            recv_sem=recv_sem.at[group],
            device_id=device,
            device_id_type=pl.DeviceIdType.MESH,
        ).start()

    def await_bytes(view, sem):
        pltpu.make_async_copy(view, view, sem).wait()

    def rows(start, size):
        return pl.ds(pl.multiple_of(start, size), size)

    ID_NEAR, ID_FAR, ID_SEQ, SLOTS, UP = range(5)
    Z0 = 5
    X0 = Z0 + ROW_PARTS
    GZ0 = X0 + ROW_PARTS
    GX0 = GZ0 + GRAD_PARTS

    def spread_all(buf, start, size, group):
        mine = rows(start + seq * size, size)
        for step in range(HEADS - 1):
            send(buf.at[mine, :], buf.at[mine, :], group, beside(step))
        leaving.append((group, buf.at[pl.ds(start, 3 * size), :]))

    def settle_all(buf, start, size, group):
        await_bytes(buf.at[pl.ds(start, 3 * size), :], recv_sem.at[group])

    owner_copy = pltpu.make_async_copy(owner_hbm, owner_v, local_sem.at[4])
    owner_copy.start()
    offset_copy = pltpu.make_async_copy(offset_hbm, offset_v, local_sem.at[5])
    offset_copy.start()
    lengths_copy = pltpu.make_async_copy(lengths_hbm, lengths, local_sem.at[6])
    lengths_copy.start()
    up_copy = pltpu.make_async_copy(up_hbm, up_all.at[rows(seq * tokens, tokens), :], local_sem.at[0])
    up_copy.start()
    table_copy = pltpu.make_async_copy(table_hbm, table, local_sem.at[1])
    table_copy.start()
    in_copy = pltpu.make_async_copy(w_in_hbm, w_in, local_sem.at[2])
    in_copy.start()
    out_copy = pltpu.make_async_copy(w_out_hbm, w_out, local_sem.at[3])
    out_copy.start()

    barrier = pltpu.get_barrier_semaphore()
    @pl.loop(0, ring - 1)
    def _(step):
        pl.semaphore_signal(barrier, inc=1, device_id=far(step), device_id_type=pl.DeviceIdType.MESH)

    for one, two in around:
        there = (z * PEERS + near_index(one), beside_index(two))
        pl.semaphore_signal(barrier, inc=1, device_id=there, device_id_type=pl.DeviceIdType.MESH)

    owner_copy.wait()
    offset_copy.wait()
    owner = owner_v[...]
    code = owner * table.shape[0] + offset_v[...]
    id_near[p] = jnp.broadcast_to(code, (8, tokens))
    id_seq[seq] = id_near[p]
    pl.semaphore_wait(barrier, len(around) + ring - 1)

    for step in range(PEERS - 1):
        send(id_near.at[p], id_near.at[p], ID_NEAR, near(step))
    leaving.append((ID_NEAR, id_near.at[pl.ds(0, PEERS - 1)]))
    for step in range(HEADS - 1):
        send(id_seq.at[seq], id_seq.at[seq], ID_SEQ, beside(step))
    leaving.append((ID_SEQ, id_seq.at[pl.ds(0, HEADS - 1)]))

    n_sub = iota((tokens, tokens), 0)
    n_lane = iota((tokens, tokens), 1)

    def both_ways(owners):
        wide = jnp.broadcast_to(owners.astype(F32), (tokens, tokens))
        return wide, wide.T

    owner_lane, owner_sub = both_ways(owner)
    second_lane = jnp.max(
        jnp.where((owner_lane == owner_sub) & (n_sub < n_lane), 1.0, 0.0), axis=0, keepdims=True
    )
    slot_lane = (owner // PEERS) * block + second_lane.astype(jnp.int32) * PEERS + owner % PEERS
    place_out = jnp.where(iota((slots, tokens), 0) == slot_lane, 1.0, 0.0).astype(BF16)

    def picker(owners):
        lane, sub = both_ways(owners)
        second = jnp.max(
            jnp.where((lane == sub) & (n_lane < n_sub), 1.0, 0.0), axis=1, keepdims=True
        ).astype(jnp.int32)
        owner_of = sub[:, :1].astype(jnp.int32)
        slot = (owner_of % PEERS) * chunk_rows + (owner_of // PEERS) * 2 + second
        return jnp.where(iota((tokens, slots), 1) == slot, 1.0, 0.0).astype(BF16)

    row_to = iota((slots, slots), 0)
    row_from = iota((slots, slots), 1)
    rest = row_to % chunk_rows
    source_row = (rest // 2) * block + (rest % 2) * PEERS + row_to // chunk_rows
    regroup = jnp.where(row_from == source_row, 1.0, 0.0).astype(BF16)

    await_bytes(id_near.at[pl.ds(0, PEERS - 1)], recv_sem.at[ID_NEAR])
    id_all[z] = jnp.concatenate([id_near[i, 0:1, :] for i in range(PEERS)], axis=0)

    @pl.loop(0, ring - 1)
    def _(step):
        send(id_all.at[z], id_all.at[z], ID_FAR, far(step))

    leaving.append((ID_FAR, id_all.at[pl.ds(0, ring - 1)]))
    up_copy.wait()
    spread_all(up_all, 0, tokens, UP)

    in_copy.wait()
    for i in range(4 * HEADS):
        columns = slice(i * head, (i + 1) * head)
        w_head[columns, :] = w_in[:, columns].T
    group = HEADS * tokens
    edge = 2 * tokens
    act[:, :edge] = jnp.zeros((4 * width, edge), BF16)
    act[:, edge + group :] = jnp.zeros((4 * width, edge), BF16)
    grad_out[:, group:] = jnp.zeros((width, edge), BF16)
    for h in range(HEADS):
        kv_rows[0, h, :edge, :] = jnp.zeros((edge, head), BF16)
        weights[h, edge:, group:] = jnp.zeros((group, edge), BF16)
        slopes[h, edge:, group:] = jnp.zeros((group, edge), F32)
        slopes[h, :edge, :group] = jnp.zeros((edge, group), F32)
    table_copy.wait()
    out_copy.wait()

    await_bytes(id_all.at[pl.ds(0, ring - 1)], recv_sem.at[ID_FAR])
    codes = id_all[...].reshape(ring * PEERS, tokens)
    wanted = (codes // table.shape[0]) == me
    offsets = (codes % table.shape[0]).astype(F32)
    place = iota((ring * PEERS, tokens), 1).astype(F32)
    first = jnp.min(jnp.where(wanted, place, 1000.0), axis=1, keepdims=True)
    last = jnp.max(jnp.where(wanted, place, -1.0), axis=1, keepdims=True)
    first_off = jnp.sum(jnp.where(place == first, offsets, 0.0), axis=1, keepdims=True)
    last_off = jnp.sum(jnp.where(place == last, offsets, 0.0), axis=1, keepdims=True)
    none = float(table.shape[0])
    first_off = jnp.where(first < 1000.0, first_off, none)
    last_off = jnp.where(last > first, last_off, none)
    row_id = iota((ring * PEERS, table.shape[0]), 1).astype(F32)

    def interleave(one, two):
        both = [x.reshape(ring, PEERS, x.shape[1]) for x in (one, two)]
        return jnp.concatenate(both, axis=1).reshape(slots, one.shape[1])

    chosen = interleave(
        jnp.where(row_id == first_off, 1.0, 0.0), jnp.where(row_id == last_off, 1.0, 0.0)
    ).astype(BF16)
    for c in range(ROW_PARTS):
        rows_out[c] = mul_nn(chosen, table[:, c * row_part : (c + 1) * row_part]).astype(BF16)
        mine = rows(z * block, block)

        @pl.loop(0, ring - 1)
        def _(step, c=c, mine=mine):
            there = rows(far_index(step) * block, block)
            send(rows_out.at[c, there, :], rows_z.at[c, mine, :], Z0 + c, far(step))

        leaving.append((Z0 + c, rows_z.at[c, pl.ds(0, slots - block), :]))

        rows_z[c, mine, :] = rows_out[c, mine, :]

    slot_off = interleave(
        jnp.broadcast_to(first_off, (ring * PEERS, tokens)),
        jnp.broadcast_to(last_off, (ring * PEERS, tokens)),
    ).T[:8]
    high = jnp.floor(slot_off * 0.0625)
    digits = jnp.concatenate([high, slot_off - 16.0 * high], axis=0).astype(BF16)
    moved = mul_nt(digits, regroup)
    slot_rows[seq] = moved[:8] * 16.0 + moved[8:]
    for step in range(HEADS - 1):
        send(slot_rows.at[seq], slot_rows.at[seq], SLOTS, beside(step))
    leaving.append((SLOTS, slot_rows.at[pl.ds(0, HEADS - 1)]))

    settle_all(up_all, 0, tokens, UP)
    grad_gated[...] = mul_nt(w_out[...], up_all[...])
    up_t[...] = up_all[rows(seq * tokens, tokens), :].astype(F32).T
    await_bytes(id_seq.at[pl.ds(0, HEADS - 1)], recv_sem.at[ID_SEQ])
    pick_in = [picker(id_seq[i, 0:1, :] // table.shape[0]) for i in range(HEADS)]

    def pass_around(c, src, src_sem, mid, dst, sem):
        await_bytes(src.at[c, pl.ds(0, slots - block), :], recv_sem.at[src_sem + c])
        mid[c] = mul_nn(regroup, src[c]).astype(BF16)
        mine = rows(seq * slots + p * chunk_rows, chunk_rows)
        for one, two in around:
            to = near_index(one)
            there = rows(to * chunk_rows, chunk_rows)
            device = (z * PEERS + to, beside_index(two))
            send(mid.at[c, there, :], dst.at[c, mine, :], sem + c, device)
        leaving.append((sem + c, dst.at[c, pl.ds(0, HEADS * slots - chunk_rows), :]))
        dst[c, mine, :] = mid[c, rows(p * chunk_rows, chunk_rows), :]

    def arrive_around(c, dst, sem):
        await_bytes(dst.at[c, pl.ds(0, HEADS * slots - chunk_rows), :], recv_sem.at[sem + c])

    for c in range(ROW_PARTS):
        pass_around(c, rows_z, Z0, rows_x, rows_in, X0)
    for c in range(ROW_PARTS):
        arrive_around(c, rows_in, X0)
        for i in range(HEADS):
            found = mul_nn(pick_in[i], rows_in[c, i * slots : (i + 1) * slots, :])
            emb_all[c, i * tokens : (i + 1) * tokens, :] = found.astype(BF16)

    own = rows(seq * tokens, tokens)
    emb_own = jnp.concatenate([emb_all[c, own, :] for c in range(ROW_PARTS)], axis=1).astype(F32)
    emb_t = emb_own.T
    centered_t = emb_t - jnp.mean(emb_t, axis=0, keepdims=True)
    inv_own = lax.rsqrt(jnp.mean(centered_t * centered_t, axis=0, keepdims=True) + EPS)
    normed_t[...] = centered_t * inv_own

    for i in range(HEADS):
        here = slice(i * tokens, (i + 1) * tokens)
        wide = jnp.concatenate([emb_all[c, here, :] for c in range(ROW_PARTS)], axis=1).astype(F32)
        centered = wide - jnp.mean(wide, axis=1, keepdims=True)
        inv = lax.rsqrt(jnp.mean(centered * centered, axis=1, keepdims=True) + EPS)
        normed_bf[here, :] = (centered * inv).astype(BF16)

    pre[...] = mul_nt(w_head[...], normed_bf[...])
    inside = slice(edge, edge + group)

    def head_of(i, h):
        return slice(i * width + h * head, i * width + (h + 1) * head)

    for i in range(4):
        for h in range(HEADS):
            x = pre[head_of(i, h), :]
            found = (x * jax.nn.sigmoid(x)).astype(BF16)
            act[head_of(i, h), inside] = found
            if i == 1:
                kv_rows[0, h, inside, :] = found.T
            if i == 3:
                kv_rows[1, h, inside, :] = found.T
    GATE, VALUE, QUERY, KEY = range(4)

    lengths_copy.wait()
    start_two = lengths[0, 0]
    start_three = start_two + lengths[0, 1]

    def user_of(position):
        return (position >= start_two).astype(jnp.int32) + (position >= start_three).astype(jnp.int32)

    scale = head ** (-0.5)
    for j in range(HEADS):
        low = max(0, j - 2) * tokens
        count = (j + 1) * tokens - low
        here = slice(j * tokens, (j + 1) * tokens)
        here_in = slice(edge + j * tokens, edge + (j + 1) * tokens)
        ms_in = slice(edge + low, edge + low + count)
        m_at = iota((count, 1), 0) + low
        n_at = iota((1, tokens), 1) + j * tokens
        allowed = (user_of(m_at) == user_of(n_at)) & (m_at <= n_at)
        for h in range(HEADS):
            scores = mul_nn(kv_rows[1, h, ms_in, :], act[head_of(QUERY, h), here_in]) * scale
            logistic = jax.nn.sigmoid(scores)
            weight = jnp.where(allowed, scores * logistic, 0.0).astype(BF16)
            weights[h, ms_in, here] = weight
            slopes[h, ms_in, here] = jnp.where(
                allowed, logistic * (1.0 + scores * (1.0 - logistic)) * scale, 0.0
            )
            attended[head_of(0, h), here] = mul_nn(act[head_of(VALUE, h), ms_in], weight)
        out = attended[:, here]
        g = grad_gated[:, here] * act[:width, here_in].astype(F32)
        out = out - jnp.mean(out, axis=0, keepdims=True)
        inv_out = lax.rsqrt(jnp.mean(out * out, axis=0, keepdims=True) + EPS)
        out = out * inv_out
        attended[:, here] = out
        slant = jnp.mean(g * out, axis=0, keepdims=True)
        grad_out[:, here] = (
            inv_out * (g - jnp.mean(g, axis=0, keepdims=True) - out * slant)
        ).astype(BF16)

    at = pl.multiple_of(seq * tokens, tokens)
    own_n = pl.ds(at, tokens)
    own_in = pl.ds(pl.multiple_of(edge + at, tokens), tokens)
    reach = pl.ds(at, 3 * tokens)
    later_in = pl.ds(pl.multiple_of(edge + at, tokens), 3 * tokens)

    def slope(part_of):
        x = pre[part_of, own_n]
        logistic = jax.nn.sigmoid(x)
        return logistic * (1.0 + x * (1.0 - logistic))

    normed_out = attended[:, own_n]
    gate = slice(0, width)
    gp_in[gate, :] = (grad_gated[:, own_n] * normed_out * slope(gate)).astype(BF16)

    def part_normed(i):
        columns = slice(i * width, (i + 1) * width)
        return mul_nn(w_in[:, columns], gp_in[columns, :])

    as_query, as_key = [], []
    for h in range(HEADS):
        score = mul_nn(kv_rows[0, h, reach, :], grad_out[head_of(0, h), own_n])
        as_query.append((score * slopes[h, reach, own_n]).astype(BF16))
        score = mul_nn(kv_rows[0, h, own_in, :], grad_out[head_of(0, h), reach])
        as_key.append((score * slopes[h, own_in, reach]).astype(BF16))
    grad_normed = part_normed(GATE)
    for h in range(HEADS):
        to = head_of(VALUE, h)
        found = mul_nt(grad_out[head_of(0, h), reach], weights[h, own_in, reach])
        gp_in[to, :] = (found * slope(to)).astype(BF16)
    grad_normed = grad_normed + part_normed(VALUE)
    for h in range(HEADS):
        to = head_of(QUERY, h)
        found = mul_nn(act[head_of(KEY, h), reach], as_query[h])
        gp_in[to, :] = (found * slope(to)).astype(BF16)
    grad_normed = grad_normed + part_normed(QUERY)
    for h in range(HEADS):
        to = head_of(KEY, h)
        found = mul_nt(act[head_of(QUERY, h), later_in], as_key[h])
        gp_in[to, :] = (found * slope(to)).astype(BF16)
    grad_normed = grad_normed + part_normed(KEY)
    normed = normed_t[...]
    grad_rows = up_t[...] + inv_own * (
        grad_normed
        - jnp.mean(grad_normed, axis=0, keepdims=True)
        - normed * jnp.mean(grad_normed * normed, axis=0, keepdims=True)
    )
    grad_rows = grad_rows.astype(BF16)
    for c in range(GRAD_PARTS):
        g_out[c] = mul_nt(place_out, grad_rows[c * grad_part : (c + 1) * grad_part]).astype(BF16)
        mine = rows(z * block, block)

        @pl.loop(0, ring - 1)
        def _(step, c=c, mine=mine):
            there = rows(far_index(step) * block, block)
            send(g_out.at[c, there, :], g_z.at[c, mine, :], GZ0 + c, far(step))

        leaving.append((GZ0 + c, g_z.at[c, pl.ds(0, slots - block), :]))

        g_z[c, mine, :] = g_out[c, mine, :]

    gated = (attended[:, own_n] * act[:width, own_in].astype(F32)).astype(BF16)
    layer_ref[...] = (emb_own + mul_nn(gated.T, w_out[...])).astype(BF16)

    await_bytes(slot_rows.at[pl.ds(0, HEADS - 1)], recv_sem.at[SLOTS])
    table_row = iota((table.shape[0], slots), 0).astype(F32)
    placed = jnp.concatenate(
        [
            jnp.where(table_row == slot_rows[i, 0:1, :], 1.0, 0.0).astype(BF16)
            for i in range(HEADS)
        ],
        axis=1,
    )

    for c in range(GRAD_PARTS):
        pass_around(c, g_z, GZ0, g_x, g_in, GX0)
    for c in range(GRAD_PARTS):
        arrive_around(c, g_in, GX0)
        grad_ref[:, c * grad_part : (c + 1) * grad_part] = mul_nn(placed, g_in[c])

    for group, view in leaving:
        await_bytes(view, send_sem.at[group])


def local(embedding_table, project_in, project_out, row_owner, row_offset, user_lengths, upstream):
    tokens = row_offset.shape[0]
    table_rows, width = embedding_table.shape
    ring = lax.axis_size("table") // PEERS
    group = tokens * HEADS
    slots = 2 * PEERS * ring
    head = width // HEADS
    vmem_spec = pl.BlockSpec(memory_space=pltpu.VMEM)
    hbm_spec = pl.BlockSpec(memory_space=pltpu.HBM)
    vmem = pltpu.VMEM
    return pl.pallas_call(
        functools.partial(kernel, ring),
        out_shape=(
            vmem((tokens, width), BF16),
            vmem((table_rows, width), F32),
        ),
        in_specs=[hbm_spec] * 7,
        out_specs=(vmem_spec, vmem_spec),
        scratch_shapes=[
            vmem((1, tokens), jnp.int32),
            vmem((1, tokens), jnp.int32),
            pltpu.SMEM((1, 3), jnp.int32),
            vmem((PEERS, 8, tokens), jnp.int32),
            vmem((HEADS, 8, tokens), jnp.int32),
            vmem((ring, PEERS, tokens), jnp.int32),
            vmem((HEADS, 8, slots), F32),
            vmem((table_rows, width), BF16),
            vmem((width, 4 * width), BF16),
            vmem((width, width), BF16),
            vmem((group, width), BF16),
            vmem((4 * width, width), BF16),
            vmem((ROW_PARTS, slots, width // ROW_PARTS), BF16),
            vmem((ROW_PARTS, slots, width // ROW_PARTS), BF16),
            vmem((ROW_PARTS, slots, width // ROW_PARTS), BF16),
            vmem((ROW_PARTS, HEADS * slots, width // ROW_PARTS), BF16),
            vmem((ROW_PARTS, group, width // ROW_PARTS), BF16),
            vmem((group, width), BF16),
            vmem((4 * width, group), F32),
            vmem((4 * width, 2 * group), BF16),
            vmem((2, HEADS, group + 2 * tokens, head), BF16),
            vmem((HEADS, group + 2 * tokens, group + 2 * tokens), BF16),
            vmem((HEADS, group + 2 * tokens, group + 2 * tokens), F32),
            vmem((width, group), F32),
            vmem((width, group), F32),
            vmem((width, group + 2 * tokens), BF16),
            vmem((4 * width, tokens), BF16),
            vmem((width, tokens), F32),
            vmem((width, tokens), F32),
            vmem((GRAD_PARTS, slots, width // GRAD_PARTS), BF16),
            vmem((GRAD_PARTS, slots, width // GRAD_PARTS), BF16),
            vmem((GRAD_PARTS, slots, width // GRAD_PARTS), BF16),
            vmem((GRAD_PARTS, HEADS * slots, width // GRAD_PARTS), BF16),
            pltpu.SemaphoreType.DMA((7,)),
            pltpu.SemaphoreType.DMA((5 + 2 * ROW_PARTS + 2 * GRAD_PARTS,)),
            pltpu.SemaphoreType.DMA((5 + 2 * ROW_PARTS + 2 * GRAD_PARTS,)),
        ],
        compiler_params=pltpu.CompilerParams(
            collective_id=0, has_side_effects=True, vmem_limit_bytes=58 * 2**20
        ),
        name="hstu_step",
    )(
        row_owner.reshape(1, tokens),
        row_offset.reshape(1, tokens),
        user_lengths,
        embedding_table,
        project_in,
        project_out,
        upstream,
    )


def solution(mesh):
    return jax.shard_map(
        local,
        mesh=mesh,
        in_specs=(
            P("table", None),
            P(),
            P(),
            P(("table", "seq"), None),
            P(("table", "seq")),
            P("table", None),
            P(("table", "seq"), None),
        ),
        out_specs=(P(("table", "seq"), None), P("table", None)),
        check_vma=False,
    )
```
